256 devices in a mesh: gx: 8 (over z), gy: 4 (over x), gz: 8 (over y, core).
Axes of the slice: x: 4, y: 4, z: 8, core: 2. Of those that a mesh axis runs over, the one named last changes fastest.
Arguments:
- positions: float32 [3, 12288, 512], P(None, ('gx', 'gy', 'gz')), may hold values from -1 to 1
- spacing: float32 [12288, 8], P(('gx', 'gy', 'gz')), may hold values from 0.0005 to 0.02
- crossings: int32 [12288, 8], P(('gx', 'gy', 'gz')), may hold values from 0 to 255, all different within a row; in each aligned block of 48 rows (0 to 47, 48 to 95, ...) at most 3 rows name the same one
- target: float32 [3, 12288], P(None, ('gx', 'gy', 'gz')), may hold values from 0 to 1
- first_weight: bfloat16 [256, 256, 60], P(('gx', 'gy', 'gz')), may hold values from -0.75 to 0.75
- head_weight: bfloat16 [256, 4, 256], P(('gx', 'gy', 'gz')), may hold values from -0.375 to 0.375
Outputs:
- rendered: float32 [3, 12288], P(None, ('gx', 'gy', 'gz'))
- first_update: float32 [256, 256, 60], P(('gx', 'gy', 'gz'))
- head_update: float32 [256, 4, 256], P(('gx', 'gy', 'gz'))
The draws below stay inside these ranges and needn't reach their ends.
Inputs may be any that keep to these rules, and one draw needn't show every extreme that they name: `crossings`: each ray crosses 8 different bricks, in no spatial pattern over the devices. Among the rays of one device no brick is crossed more than 3 times, a bound that some block reaches.
All inputs are finite; a program needn't handle non-finite values.
Results may differ from the reference program's by a relative error of at most 0.0029.
Values sent between devices are 32-bit elements; how exact they have to be, the bound alone decides.
No kernel may reach another device: no remote copies, remote signals or barrier semaphores. Data moves between devices by JAX's collectives and lax.ppermute only.
A program may use at most 64 MiB of HBM per device.

```python
import math
import jax
import jax.numpy as jnp
import numpy as np
from jax import lax

W = 256
FREQS = 10
SAMPLES = 64
SEGS = 8
RAY_DEV = 48
BRICKS = 256
RAYS = 12288
CAP = 3
DEVICES = 256


def block_scale(own_key, dims, pieces, low, top_value):
    gain = 1.0
    for position, shards_of in pieces:
        heights = jax.random.uniform(jax.random.fold_in(jax.random.fold_in(own_key, 6), position), (shards_of,), jnp.float32, low / len(pieces), top_value / len(pieces))
        gain = gain * jnp.repeat(jnp.exp(heights), dims[position] // shards_of).reshape((-1,) + (1,) * (len(dims) - 1 - position))
    return gain


def deal_out(rng, own, number, rows, number_of, top, limit, lean):
    order = jax.random.permutation(rng, number_of)
    heavy_load, common = load_shares(number_of, rows * top, limit, lean, True), load_shares(number_of, rows * top, limit, lean, False)
    places = jnp.arange(number_of)

    def named(tallies, turn):
        used = int((tallies > 0).sum())
        fixed = max(1, used // 4)
        moved = fixed + (places - fixed + turn * (used - fixed)) % max(1, number_of - fixed)
        return jnp.zeros((number_of,), jnp.int32).at[order[jnp.where(places < fixed, places, moved)]].set(jnp.asarray(tallies, jnp.int32))

    tallies = jnp.where(number % 4 == 0, named(heavy_load, number // 4), named(common, number - number // 4 - 1))
    mixed = jax.random.permutation(jax.random.fold_in(own, 3), number_of)
    donor, receiver = mixed[0:number_of // 2 * 2:2], mixed[1:number_of // 2 * 2:2]
    room = jnp.minimum(tallies[donor] - 1, limit - tallies[receiver]) // 2
    room = jnp.where((donor == order[0]) | (receiver == order[0]) | (tallies[receiver] == 0), 0, jnp.maximum(room, 0))
    moved = jax.random.randint(jax.random.fold_in(own, 4), (number_of // 2,), 0, 1 << 20) % (room + 1)
    tallies = tallies.at[donor].add(-moved).at[receiver].add(moved)
    labels = jnp.searchsorted(jnp.cumsum(tallies), jnp.arange(rows * top), side="right").astype(jnp.int32)
    listing = labels.reshape(top, rows).T
    listing = listing[jax.random.permutation(jax.random.fold_in(own, 1), rows)]
    turn = jax.random.randint(jax.random.fold_in(own, 2), (rows, 1), 0, top)
    return jnp.take_along_axis(listing, (jnp.arange(top)[None, :] + turn) % top, axis=1)


def load_shares(amount, total, bound, lean, full):
    portions = [(1 << 20) // math.isqrt(standing ** lean) + 1 for standing in range(1, amount + 1)]
    largest = bound if full else min(bound, max(-(-total // amount), total * portions[0] // sum(portions)))
    least = 1 if total - largest >= amount - 1 else 0
    counts, rest = [largest] + [least] * (amount - 1), total - largest - least * (amount - 1)
    while rest > 0:
        free = [i for i in range(1, amount) if counts[i] < largest] or [i for i in range(1, amount) if counts[i] < bound]
        mass, left = sum([portions[i] for i in free]), rest
        for i in free:
            addition = min(bound - counts[i], max(1, left * portions[i] // mass), rest)
            counts[i] = counts[i] + addition
            rest = rest - addition
    return np.array(counts)


def bell_draw(own_key, extent, scale, most, split=(), kind=jnp.bfloat16):
    values = jax.random.normal(own_key, extent, jnp.float32) * scale
    if len(split) > 0:
        values = block_scale(own_key, extent, split, -0.22, 0.18) * values
    return jnp.clip(values, min=-most, max=most).astype(kind)


def setup_inputs(seed: int = 0) -> dict:
    keys = jax.random.split(jax.random.key(seed), 7)
    positions = jnp.clip(jax.random.uniform(keys[0], (3, RAYS, SEGS * SAMPLES), jnp.float32, -1.0, 1.0) * block_scale(keys[0], (3, RAYS, SEGS * SAMPLES), ((1, 256),), -0.4, 0.0), -1.0, 1.0)
    spacing = jnp.clip(jnp.exp(math.log(0.02) - 3.6888794 * jax.random.uniform(keys[1], (RAYS, SEGS), jnp.float32) ** block_scale(keys[1], (RAYS, SEGS), ((0, 256),), -0.2, 0.2)), 0.0005, 0.02)
    crossings_keys = jax.random.split(jax.random.fold_in(keys[2], 1), RAYS // RAY_DEV)
    crossings_turns = jax.random.permutation(jax.random.fold_in(keys[2], 3), RAYS // RAY_DEV)
    crossings = jax.vmap(lambda own, number: deal_out(jax.random.fold_in(keys[2], 2), own, number, RAY_DEV, DEVICES, SEGS, CAP, 2))(crossings_keys, crossings_turns).reshape((RAYS, SEGS))
    target = jnp.clip(1.0 * jax.random.uniform(keys[3], (3, RAYS), jnp.float32) ** block_scale(keys[3], (3, RAYS), ((1, 256),), -0.2, 0.2), 0.0, 1.0)
    first_weight = bell_draw(keys[4], (BRICKS, W, 6 * FREQS), (6 * FREQS) ** -0.5, 0.75, ((0, 256),))
    head_weight = bell_draw(keys[5], (BRICKS, 4, W), W ** -0.5, 0.375, ((0, 256),))
    return {"positions": positions, "spacing": spacing, "crossings": crossings, "target": target, "first_weight": first_weight, "head_weight": head_weight}


PI_VALUE = 3.141592653589793
NORM_EPS = 1e-06

def encode(points):
    scales = 2.0 ** jnp.arange(FREQS, dtype=jnp.float32) * PI_VALUE
    angles = scales[:, None, None] * points[None]
    wave_table = jnp.stack([jnp.sin(angles), jnp.cos(angles)], axis=1)
    return wave_table.reshape(6 * FREQS, points.shape[1]).astype(jnp.bfloat16)

def network(first_local, head_local, points):
    encoded = encode(points)
    before = jnp.dot(first_local, encoded, preferred_element_type=jnp.float32)
    hidden = jax.nn.silu(before).astype(jnp.bfloat16)
    output = jnp.dot(head_local, hidden, preferred_element_type=jnp.float32)
    return (encoded, before, hidden, output)

def activate(output):
    return (jax.nn.softplus(output[0]), jax.nn.sigmoid(output[1:]))

def segment_forward(density, colour, step_len):
    optical = density * step_len[:, None]
    inclusive = jnp.cumsum(optical, axis=1)
    leaving = jnp.exp(-inclusive)
    weight = jnp.exp(optical - inclusive) - leaving
    seg_colour = lax.optimization_barrier(jnp.sum(weight[None] * colour, axis=2))
    return (seg_colour, leaving[:, -1], weight, leaving)

def segment_backward(colour, weight, leaving, step_len, grad_colour, grad_trans):
    shading = lax.optimization_barrier(jnp.sum(colour * grad_colour[:, :, None], axis=0))
    weighted = weight * shading
    after = lax.optimization_barrier(jnp.sum(weighted, axis=1, keepdims=True)) - jnp.cumsum(weighted, axis=1)
    grad_depth = shading * leaving - after - (grad_trans * leaving[:, -1])[:, None]
    grad_density = grad_depth * step_len[:, None]
    grad_sample = weight[None] * grad_colour[:, :, None]
    return (grad_density, grad_sample)

def ray_level(seg_colour, seg_trans, target):
    seg_total = seg_trans.shape[1]
    through = jnp.cumprod(seg_trans, axis=1)
    prefix = jnp.concatenate([jnp.ones_like(seg_trans[:, :1]), through[:, :-1]], axis=1)
    rendered = lax.optimization_barrier(jnp.sum(prefix[None] * seg_colour, axis=2))
    residual = rendered - target
    grad_colour = prefix[None] * residual[:, :, None]
    behind_list = [jnp.zeros_like(rendered)]
    for offset in range(seg_total - 1, 0, -1):
        behind_list.append(seg_colour[:, :, offset] + seg_trans[:, offset][None] * behind_list[-1])
    behind = jnp.stack(behind_list[::-1], axis=2)
    grad_trans = prefix * lax.optimization_barrier(jnp.sum(behind * residual[:, :, None], axis=0))
    return (rendered, grad_colour, grad_trans)

def output_grad(output, grad_density, grad_sample):
    colour = jax.nn.sigmoid(output[1:])
    first_row = grad_density * jax.nn.sigmoid(output[0])
    others = grad_sample * colour * (1.0 - colour)
    return jnp.concatenate([first_row[None], others], axis=0).astype(jnp.bfloat16)

def network_grad(head_local, encoded, before, hidden, upstream):
    grad_head = jnp.dot(upstream, hidden.T, preferred_element_type=jnp.float32)
    grad_hidden = jnp.dot(head_local.T, upstream, preferred_element_type=jnp.float32)
    logistic = jax.nn.sigmoid(before)
    grad_before = (grad_hidden * logistic * (1.0 + before * (1.0 - logistic))).astype(jnp.bfloat16)
    grad_first = jnp.dot(grad_before, encoded.T, preferred_element_type=jnp.float32)
    return (grad_first, grad_head)

def reference(positions, spacing, crossings, target, first_weight, head_weight):
    entries = RAY_DEV * SEGS
    brick_ids = crossings.reshape(BRICKS, entries)
    order_rank = jnp.arange(entries, dtype=jnp.int32)

    def rank_row(row):
        earlier = (row[:, None] == row[None, :]) & (order_rank[None, :] < order_rank[:, None])
        return lax.optimization_barrier(jnp.sum(earlier.astype(jnp.int32), axis=1))
    local_slot = jax.vmap(rank_row)(brick_ids).astype(jnp.int32)
    owner_ids = jnp.arange(BRICKS, dtype=jnp.int32)[:, None]
    column = ((brick_ids * BRICKS + owner_ids) * CAP + local_slot).reshape(RAYS * SEGS).astype(jnp.int32)
    brick_slots = BRICKS * CAP
    all_slots = BRICKS * brick_slots
    all_points = jnp.zeros((3, all_slots, SAMPLES), jnp.float32).at[:, column, :].set(positions.reshape(3, RAYS * SEGS, SAMPLES))
    brick_points = all_points.reshape(3, BRICKS, brick_slots * SAMPLES).transpose(1, 0, 2)

    def brick_forward(inputs):
        first_local, head_local, points = inputs
        return network(first_local, head_local, points)[3]
    outputs = lax.map(brick_forward, (first_weight, head_weight, brick_points))
    entry_out = outputs.reshape(BRICKS, 4, brick_slots, SAMPLES).transpose(1, 0, 2, 3).reshape(4, all_slots, SAMPLES)[:, column, :]
    density, colour = activate(entry_out)
    steps_all = spacing.reshape(RAYS * SEGS)
    seg_colour, seg_trans, weight, leaving = segment_forward(density, colour, steps_all)
    rendered, grad_colour, grad_trans = ray_level(seg_colour.reshape(3, RAYS, SEGS), seg_trans.reshape(RAYS, SEGS), target)
    grad_density, grad_sample = segment_backward(colour, weight, leaving, steps_all, grad_colour.reshape(3, RAYS * SEGS), grad_trans.reshape(RAYS * SEGS))
    upstream = output_grad(entry_out, grad_density, grad_sample)
    brick_upstream = jnp.zeros((4, all_slots, SAMPLES), jnp.bfloat16).at[:, column, :].set(upstream)
    brick_upstream = brick_upstream.reshape(4, BRICKS, brick_slots * SAMPLES).transpose(1, 0, 2)

    def brick_backward(inputs):
        first_local, head_local, points, upstream_local = inputs
        encoded, before, hidden, output = network(first_local, head_local, points)
        return network_grad(head_local, encoded, before, hidden, upstream_local)
    grad_first, grad_head = lax.map(brick_backward, (first_weight, head_weight, brick_points, brick_upstream))
    overall = jnp.sum(grad_first * grad_first) + jnp.sum(grad_head * grad_head)
    scale = lax.rsqrt(overall / (BRICKS * W * (6 * FREQS + 4)) + NORM_EPS)
    return (rendered, grad_first * scale, grad_head * scale)
```

```python
import jax
import jax.numpy as jnp
from jax import lax
from jax.experimental import pallas as pl
from jax.experimental.pallas import tpu as pltpu
from jax.sharding import PartitionSpec as P

FREQS = 10
SAMPLES = 64
SEGS = 8
CAP = 3
NORM_EPS = 1e-06

RAYS = 48
GROUP = 8
PEERS = 32
SLOTS = GROUP * CAP
PAIRS = SLOTS // 2
ROWS = PEERS // 2
TILE = PEERS * SAMPLES
ENTRIES = RAYS * SEGS
STEP_ROW = 3 * PAIRS
WIRE = 40
HIDDEN = 256
FORWARD_CHUNK = 1024
BACKWARD_CHUNK = 256
VMEM = 56 * 1024 * 1024
ALL = ("gx", "gy", "gz")
PEER_AXES = ("gx", "gy")

SIN_TERMS = (
    6.283185160116253,
    -41.34165503574907,
    81.60100428250003,
    -76.54978619700827,
    39.536730859838705,
)

f32 = jnp.float32
bf16 = jnp.bfloat16


def iota(shape, dim):
    return lax.broadcasted_iota(jnp.int32, shape, dim)


def exact_dot(a, b):
    return jnp.dot(a, b, preferred_element_type=f32, precision=lax.Precision.HIGHEST)


def nt_dot(a, b, precision=None):
    return lax.dot_general(
        a, b, (((1,), (1,)), ((), ())), preferred_element_type=f32, precision=precision
    )


def matrix_cost(tile_passes):
    return pl.CostEstimate(
        flops=tile_passes * 2 * HIDDEN * HIDDEN * TILE, bytes_accessed=4 << 20, transcendentals=0
    )


def split3(x):
    high = x.astype(bf16)
    rest = x - high.astype(f32)
    mid = rest.astype(bf16)
    return high, mid, (rest - mid.astype(f32)).astype(bf16)


def pick(one_hot, x):
    high, mid, low = split3(x)
    total = jnp.dot(one_hot, low, preferred_element_type=f32)
    total += jnp.dot(one_hot, mid, preferred_element_type=f32)
    return total + jnp.dot(one_hot, high, preferred_element_type=f32)


def column_of(rows_ref):
    rows = rows_ref[...].astype(f32)
    padded = jnp.concatenate([rows, jnp.zeros((SEGS, 128 - RAYS), f32)], axis=1).T
    return jnp.concatenate([padded[:RAYS, s : s + 1] for s in range(SEGS)], axis=0)


def pack_kernel(own_ref, pos_ref, step_ref, cross_ref, send_ref, index_ref, dest_ref, data_ref):
    brick_col = column_of(cross_ref)
    step_col = column_of(step_ref)
    sub = iota((ENTRIES, ENTRIES), 0)
    lane = iota((ENTRIES, ENTRIES), 1)
    brick_row = jnp.sum(jnp.where(sub == lane, brick_col, 0.0), axis=0, keepdims=True)
    same = brick_col == brick_row
    rank_col = jnp.sum(jnp.where(same & (lane < sub), 1.0, 0.0), axis=1, keepdims=True)
    rank_row = jnp.sum(jnp.where(same & (sub < lane), 1.0, 0.0), axis=0, keepdims=True)
    own = own_ref[0]

    def place(number, rank):
        dest = jnp.floor(number * (1.0 / GROUP))
        member = (number - GROUP * dest).astype(jnp.int32) ^ own
        return dest, member.astype(f32) * CAP + rank

    dest_col, slot_col = place(brick_col, rank_col)
    dest_row, slot_row = place(brick_row, rank_row)
    pair_row = jnp.floor(slot_row * 0.5)
    half_row = slot_row - 2.0 * pair_row
    half_row = jnp.where(own_ref[1] < ROWS, half_row, 1.0 - half_row)
    target_row = pair_row * PEERS + dest_row
    here = sub.astype(f32) == target_row
    one_hot = jnp.concatenate(
        [jnp.where(here & (half_row == half), 1.0, 0.0).astype(bf16) for half in (0.0, 1.0)], axis=1
    )
    left = iota((RAYS, 128), 1) < SAMPLES
    for c in range(3):
        for q in range(SEGS // 2):
            x = pos_ref[c, :, 128 * q : 128 * q + 128]
            y = pltpu.roll(x, SAMPLES, 1)
            blocks = (
                (0, 2 * q, jnp.where(left, x, 0.0)),
                (0, 2 * q + 1, jnp.where(left, y, 0.0)),
                (1, 2 * q, jnp.where(left, 0.0, y)),
                (1, 2 * q + 1, jnp.where(left, 0.0, x)),
            )
            for half, s, block in blocks:
                row = half * ENTRIES + s * RAYS
                for part, value in enumerate(split3(block)):
                    data_ref[part, row : row + RAYS, 128 * c : 128 * c + 128] = value
    total = jnp.dot(one_hot, data_ref[2], preferred_element_type=f32)
    total += jnp.dot(one_hot, data_ref[1], preferred_element_type=f32)
    total += jnp.dot(one_hot, data_ref[0], preferred_element_type=f32)
    for pair in range(PAIRS):
        for c in range(3):
            send_ref[:, 3 * pair + c, :] = total[
                pair * PEERS : (pair + 1) * PEERS, 128 * c : 128 * c + 128
            ]
    to_dest = jnp.where(iota((PEERS, ENTRIES), 0).astype(f32) == dest_row, 1.0, 0.0)
    lane_128 = iota((ENTRIES, 128), 1)
    by_slot = jnp.where(lane_128.astype(f32) == slot_col, step_col, 0.0)
    send_ref[:, STEP_ROW, :] = pick(to_dest.astype(bf16), by_slot)
    send_ref[:, STEP_ROW + 1 :, :] = jnp.zeros((PEERS, WIRE - STEP_ROW - 1, 128), f32)
    index_ref[...] = jnp.where(lane_128 < 64, dest_col, slot_col)
    dest_ref[...] = jnp.broadcast_to(dest_row, (8, ENTRIES))


def pack(own, positions, spacing, crossings):
    vmem = pl.BlockSpec(memory_space=pltpu.VMEM)
    return pl.pallas_call(
        pack_kernel,
        out_shape=(
            jax.ShapeDtypeStruct((PEERS, WIRE, 128), f32),
            jax.ShapeDtypeStruct((ENTRIES, 128), f32),
            jax.ShapeDtypeStruct((8, ENTRIES), f32),
        ),
        in_specs=[pl.BlockSpec(memory_space=pltpu.SMEM), vmem, vmem, vmem],
        out_specs=(vmem, vmem, vmem),
        scratch_shapes=[pltpu.VMEM((3, 2 * ENTRIES, 384), bf16)],
        compiler_params=pltpu.CompilerParams(vmem_limit_bytes=VMEM),
        name="pack",
    )(own, positions, spacing, crossings)


def wave_constants():
    row = iota((64, 128), 0)
    k = row // 6
    within = row - 6 * k
    real = row < 6 * FREQS
    half_scale = jnp.where(real, 0.5, 0.0)
    for step in range(FREQS - 1):
        half_scale = jnp.where(k > step, half_scale * 2.0, half_scale)
    offset = jnp.where(real & (within >= 3), 0.0, 0.25)
    component = jnp.where(within >= 3, within - 3, within)
    component = component[:24]
    return half_scale, offset, component == 0, component == 1


def encode_into(enc_ref, recv_ref, slot, constants):
    half_scale, offset, first, second = constants
    pair = slot // 2
    near_side = (iota((8, 128), 1) < SAMPLES) == (slot == 2 * pair)
    for r in range(ROWS):
        p0, p1, p2 = [
            jnp.where(
                near_side,
                jnp.broadcast_to(recv_ref[r, pl.ds(3 * pair + c, 1), :], (8, 128)),
                jnp.broadcast_to(recv_ref[r + ROWS, pl.ds(3 * pair + c, 1), :], (8, 128)),
            )
            for c in range(3)
        ]
        p0, p1, p2 = [jnp.concatenate([p] * 3, axis=0) for p in (p0, p1, p2)]
        point = jnp.where(first, p0, jnp.where(second, p1, p2))
        point = jnp.concatenate([point, point, point[:16]], axis=0)
        turns = point * half_scale
        turns = turns - jnp.round(turns)
        y = 0.25 - jnp.abs(turns - offset)
        y = jnp.maximum(y, -0.5 - y)
        z = y * y
        value = SIN_TERMS[-1]
        for term in SIN_TERMS[-2::-1]:
            value = value * z + term
        enc_ref[:, 128 * r : 128 * r + 128] = (value * y).astype(bf16)


def spread(near, far, slot, lane_index):
    near_side = (iota((ROWS, 128), 1) < SAMPLES) == (slot % 2 == 0)
    return jnp.where(
        near_side, near[:, lane_index : lane_index + 1], far[:, lane_index : lane_index + 1]
    )


def same_half():
    i = iota((128, 128), 0)
    j = iota((128, 128), 1)
    return i, j, (i < SAMPLES) == (j < SAMPLES)


def as_matrix(mask):
    return jnp.where(mask, 1.0, 0.0)


def forward_kernel(*refs):
    recv_ref = refs[0]
    weight_refs = refs[1 : 1 + GROUP]
    small_ref, saved_ref, step_ref, used_ref = refs[1 + GROUP : 5 + GROUP]
    w_ref, head_ref, enc_ref, out_ref = refs[5 + GROUP :]

    for i in range(GROUP):
        packed = weight_refs[i][...]
        w_ref[i] = (0.5 * packed).T.astype(bf16)
        head_ref[i] = packed[48:64].astype(bf16)

    near = recv_ref[:ROWS, STEP_ROW, :]
    far = recv_ref[ROWS:, STEP_ROW, :]
    most = jnp.max(jnp.maximum(near, far), axis=0, keepdims=True)
    count = jnp.int32(0)
    for slot in range(SLOTS):
        if slot == SLOTS // 2:
            used_ref[SLOTS] = count
        used_ref[count] = slot
        count += (most[0, slot] > 0.0).astype(jnp.int32)
    used_ref[SLOTS + 1] = count
    for slot in range(SLOTS):
        step_ref[slot] = spread(near, far, slot, slot)
    out_ref[...] = jnp.zeros((4, SLOTS, ROWS, 128), f32)

    constants = wave_constants()

    def turn(number, carry):
        slot = used_ref[number]
        brick = slot // CAP
        encode_into(enc_ref, recv_ref, slot, constants)
        first = w_ref[brick]
        head = head_ref[brick]
        for n in range(TILE // FORWARD_CHUNK):
            half = jnp.dot(
                first, enc_ref[:, n * FORWARD_CHUNK : (n + 1) * FORWARD_CHUNK], preferred_element_type=f32
            )
            hidden = (half + half * jnp.tanh(half)).astype(bf16)
            output = jnp.dot(head, hidden, preferred_element_type=f32)
            for r in range(FORWARD_CHUNK // 128):
                row = n * (FORWARD_CHUNK // 128) + r
                for v in range(4):
                    out_ref[v, slot, row : row + 1, :] = output[
                        12 + v : 13 + v, 128 * r : 128 * r + 128
                    ]
        return carry

    lax.fori_loop(0, count, turn, 0)

    rows = SLOTS * ROWS
    i, j, same = same_half()
    until = as_matrix(same & (i <= j))
    outputs = [out_ref[v].reshape(rows, 128) for v in range(4)]
    steps = step_ref[...].reshape(rows, 128)
    raw = outputs[0]
    density = jnp.maximum(raw, 0.0) + jnp.log1p(jnp.exp(-jnp.abs(raw)))
    optical = density * steps
    inclusive = exact_dot(optical, until)
    leaving = jnp.exp(-inclusive)
    weight = jnp.exp(optical - inclusive) - leaving
    saved_ref[3] = jax.nn.sigmoid(raw).reshape(SLOTS, ROWS, 128)
    saved_ref[4] = weight.reshape(SLOTS, ROWS, 128)
    saved_ref[5] = leaving.reshape(SLOTS, ROWS, 128)
    total = as_matrix(((i < SAMPLES) & (j == 0)) | ((i >= SAMPLES) & (j == 1)))
    last = as_matrix(((i == SAMPLES - 1) & (j == 0)) | ((i == 127) & (j == 1)))
    results = []
    for v in range(3):
        colour = jax.nn.sigmoid(outputs[1 + v])
        saved_ref[v] = colour.reshape(SLOTS, ROWS, 128)
        results.append(exact_dot(weight * colour, total))
    results.append(exact_dot(leaving, last))
    lane = iota((ROWS, 128), 1)
    for side in range(2):
        gathered = jnp.zeros((ROWS, 128), f32)
        for v in range(4):
            for slot in range(SLOTS):
                half = (side + slot) % 2
                column = results[v][slot * ROWS : (slot + 1) * ROWS, half : half + 1]
                gathered = jnp.where(lane == v * SLOTS + slot, column, gathered)
        small_ref[side * ROWS : (side + 1) * ROWS, :] = gathered


def forward(received, weights):
    vmem = pl.BlockSpec(memory_space=pltpu.VMEM)
    return pl.pallas_call(
        forward_kernel,
        out_shape=(
            jax.ShapeDtypeStruct((PEERS, 128), f32),
            jax.ShapeDtypeStruct((6, SLOTS, ROWS, 128), f32),
            jax.ShapeDtypeStruct((SLOTS, ROWS, 128), f32),
            jax.ShapeDtypeStruct((SLOTS + 2,), jnp.int32),
        ),
        in_specs=[vmem] * (1 + GROUP),
        out_specs=(vmem, vmem, vmem, pl.BlockSpec(memory_space=pltpu.SMEM)),
        scratch_shapes=[
            pltpu.VMEM((GROUP, HIDDEN, 64), bf16),
            pltpu.VMEM((GROUP, 16, HIDDEN), bf16),
            pltpu.VMEM((64, TILE), bf16),
            pltpu.VMEM((4, SLOTS, ROWS, 128), f32),
        ],
        compiler_params=pltpu.CompilerParams(vmem_limit_bytes=VMEM),
        cost_estimate=matrix_cost(SLOTS * 2),
        name="forward",
    )(received, *weights)


def ray_kernel(small_ref, index_ref, dest_ref, target_ref, grads_ref, rendered_ref):
    lane = iota((ENTRIES, 128), 1)
    value = lane // SLOTS
    slot = (lane - value * SLOTS).astype(f32)
    dest_col = index_ref[:, 0:1]
    slot_col = index_ref[:, 64:65]
    to_entry = jnp.where(lane.astype(f32) == dest_col, 1.0, 0.0)
    small = jnp.concatenate([small_ref[...], jnp.zeros((128 - PEERS, 128), f32)], axis=0)
    mine = (slot == slot_col) & (value < 4)
    found = jnp.where(mine, exact_dot(to_entry, small), 0.0)
    i = iota((128, 128), 0)
    j = iota((128, 128), 1)
    segments = exact_dot(found, as_matrix((i // SLOTS == j) & (j < 4)))

    lane = iota((RAYS, 128), 1)
    parts = [segments[s * RAYS : (s + 1) * RAYS] for s in range(SEGS)]
    trans = [jnp.broadcast_to(part[:, 3:4], (RAYS, 128)) for part in parts]
    prefix = [jnp.ones((RAYS, 128), f32)]
    for s in range(SEGS - 1):
        prefix.append(prefix[s] * trans[s])
    rendered = prefix[0] * parts[0]
    for s in range(1, SEGS):
        rendered += prefix[s] * parts[s]
    residual = jnp.where(lane < 3, rendered - target_ref[...], 0.0)
    behind = jnp.zeros((RAYS, 128), f32)
    grads = [None] * SEGS
    for s in range(SEGS - 1, -1, -1):
        through = prefix[s] * jnp.sum(behind * residual, axis=1, keepdims=True)
        grads[s] = jnp.where(lane == 3, through, prefix[s] * residual)
        behind = parts[s] + trans[s] * behind
    spread_back = exact_dot(jnp.concatenate(grads, axis=0), as_matrix((j // SLOTS == i) & (i < 4)))
    to_dest = jnp.where(iota((PEERS, ENTRIES), 0).astype(f32) == dest_ref[0:1, :], 1.0, 0.0)
    grads_ref[...] = exact_dot(to_dest, jnp.where(mine, spread_back, 0.0))
    eye = as_matrix(iota((8, 128), 0) == iota((8, 128), 1))
    rendered_ref[...] = nt_dot(eye, rendered, lax.Precision.HIGHEST)[0:3]


def ray_level(small, index, dest, target):
    return pl.pallas_call(
        ray_kernel,
        out_shape=(
            jax.ShapeDtypeStruct((PEERS, 128), f32),
            jax.ShapeDtypeStruct((3, RAYS), f32),
        ),
        compiler_params=pltpu.CompilerParams(vmem_limit_bytes=VMEM),
        name="rays",
    )(small, index, dest, target)


def upstream_into(up_ref, grads_ref, saved_ref, step_ref):
    near = grads_ref[:ROWS]
    far = grads_ref[ROWS:]
    for v in range(4):
        for slot in range(SLOTS):
            up_ref[v, slot] = spread(near, far, slot, v * SLOTS + slot)

    rows = SLOTS * ROWS

    def flat(x):
        return x.reshape(rows, 128)

    i, j, same = same_half()
    beyond = as_matrix(same & (i > j))
    last = as_matrix(same & ((i == SAMPLES - 1) | (i == 127)))
    weight = flat(saved_ref[4])
    leaving = flat(saved_ref[5])
    shading = flat(saved_ref[0]) * flat(up_ref[0])
    shading += flat(saved_ref[1]) * flat(up_ref[1])
    shading += flat(saved_ref[2]) * flat(up_ref[2])
    after = exact_dot(weight * shading, beyond)
    grad_depth = shading * leaving - after - flat(up_ref[3]) * exact_dot(leaving, last)
    upstream = [grad_depth * flat(step_ref[...]) * flat(saved_ref[3])]
    for v in range(3):
        colour = flat(saved_ref[v])
        upstream.append(weight * flat(up_ref[v]) * colour * (1.0 - colour))
    for v in range(4):
        up_ref[v] = upstream[v].reshape(SLOTS, ROWS, 128)


def gradients(low, up_ref, recv_ref, used_ref, weight_refs, total_refs, scratch):
    w_ref, back_ref, enc_ref, row_ref = scratch
    for i, ref in enumerate(weight_refs):
        packed = 0.5 * ref[...]
        w_ref[i] = packed.T.astype(bf16)
        back_ref[i] = packed[48:64].T.astype(bf16)
    total_refs[...] = jnp.zeros(total_refs.shape, f32)
    row_ref[...] = jnp.zeros((16, TILE), f32)
    constants = wave_constants()

    def turn(number, carry):
        slot = used_ref[number]
        brick = slot // CAP - low
        encode_into(enc_ref, recv_ref, slot, constants)
        for v in range(4):
            rows_v = up_ref[v, slot]
            for r in range(ROWS):
                row_ref[12 + v : 13 + v, 128 * r : 128 * r + 128] = rows_v[r : r + 1, :]
        first = w_ref[brick]
        back = back_ref[brick]
        grad_first = jnp.zeros((64, HIDDEN), f32)
        grad_head = jnp.zeros((16, HIDDEN), f32)
        for n in range(TILE // BACKWARD_CHUNK):
            lanes = slice(n * BACKWARD_CHUNK, (n + 1) * BACKWARD_CHUNK)
            encoded = enc_ref[:, lanes]
            up = row_ref[:, lanes].astype(bf16)
            half = jnp.dot(first, encoded, preferred_element_type=f32)
            grad_hidden = jnp.dot(back, up, preferred_element_type=f32)
            bend = jnp.tanh(half)
            product = half * bend
            hidden = (half + product).astype(bf16)
            slope = (1.0 + bend) * ((1.0 + half) - product)
            grad_before = (grad_hidden * slope).astype(bf16)
            grad_first += nt_dot(encoded, grad_before)
            grad_head += nt_dot(up, hidden)
        total_refs[brick] += grad_first
        total_refs[brick, 48:64] += grad_head
        return carry

    if low:
        lax.fori_loop(used_ref[SLOTS], used_ref[SLOTS + 1], turn, 0)
    else:
        lax.fori_loop(0, used_ref[SLOTS], turn, 0)


HALF = GROUP // 2


def far_kernel(*refs):
    grads_ref, saved_ref, step_ref, recv_ref, used_ref = refs[:5]
    weight_refs = refs[5 : 5 + HALF]
    up_ref = refs[5 + HALF]
    total_refs = refs[6 + HALF : 6 + 2 * HALF]
    sum_ref = refs[6 + 2 * HALF]
    upstream_into(up_ref, grads_ref, saved_ref, step_ref)
    gradients(HALF, up_ref, recv_ref, used_ref, weight_refs, sum_ref, refs[7 + 2 * HALF :])
    for i in range(HALF):
        total_refs[i][...] = sum_ref[i]


def near_kernel(*refs):
    up_ref, recv_ref, used_ref = refs[:3]
    weight_refs = refs[3 : 3 + HALF]
    total_refs = refs[3 + HALF : 3 + 2 * HALF]
    sum_ref = refs[3 + 2 * HALF]
    gradients(0, up_ref, recv_ref, used_ref, weight_refs, sum_ref, refs[4 + 2 * HALF :])
    for i in range(HALF):
        total_refs[i][...] = sum_ref[i]


def backward_call(kernel, name, extra, operands, dense):
    vmem = pl.BlockSpec(memory_space=pltpu.VMEM)
    smem = pl.BlockSpec(memory_space=pltpu.SMEM)
    totals = tuple(jax.ShapeDtypeStruct((64, HIDDEN), f32) for _ in range(HALF))
    return pl.pallas_call(
        kernel,
        out_shape=extra + totals,
        in_specs=[vmem] * dense + [smem] + [vmem] * HALF,
        out_specs=tuple([vmem] * (len(extra) + HALF)),
        scratch_shapes=[
            pltpu.VMEM((HALF, 64, HIDDEN), f32),
            pltpu.VMEM((HALF, HIDDEN, 64), bf16),
            pltpu.VMEM((HALF, HIDDEN, 16), bf16),
            pltpu.VMEM((64, TILE), bf16),
            pltpu.VMEM((16, TILE), f32),
        ],
        compiler_params=pltpu.CompilerParams(vmem_limit_bytes=VMEM),
        cost_estimate=matrix_cost(SLOTS // 2 * 4),
        name=name,
    )(*operands)


def backward_far(grads, saved, steps, received, used, weights):
    dense = (jax.ShapeDtypeStruct((4, SLOTS, ROWS, 128), f32),)
    operands = (grads, saved, steps, received, used, *weights)
    return backward_call(far_kernel, "backward_far", dense, operands, 4)


def backward_near(upstream, received, used, weights):
    return backward_call(near_kernel, "backward_near", (), (upstream, received, used, *weights), 2)


def sum_kernel(*refs):
    total = refs[0][...]
    for ref in refs[1:GROUP]:
        total += ref[...]
    refs[GROUP][...] = total
    square = jnp.sum(jnp.sum(total * total, axis=1, keepdims=True), axis=0, keepdims=True)
    refs[GROUP + 1][...] = jnp.broadcast_to(square, refs[GROUP + 1].shape)


def add_up(partials, bricks):
    return pl.pallas_call(
        sum_kernel,
        out_shape=(
            jax.ShapeDtypeStruct((64, HIDDEN), f32),
            jax.ShapeDtypeStruct((bricks, 128), f32),
        ),
        name="add_up",
    )(*partials)


def normalize(total, squares, count):
    def body(total_ref, squares_ref, first_ref, head_ref):
        overall = jnp.sum(squares_ref[:, 0:1], axis=0, keepdims=True)
        scaled = total_ref[...] * lax.rsqrt(overall / count + NORM_EPS)
        first_ref[:, 0, :] = scaled[: 6 * FREQS]
        head_ref[0] = scaled[6 * FREQS :]

    first, head = pl.pallas_call(
        body,
        out_shape=(
            jax.ShapeDtypeStruct((6 * FREQS, 1, HIDDEN), f32),
            jax.ShapeDtypeStruct((1, 4, HIDDEN), f32),
        ),
        name="normalize",
    )(total, squares)
    return first.transpose(1, 2, 0), head


def with_member(x, difference):
    return lax.ppermute(x, "gz", [(i, i ^ difference) for i in range(GROUP)])


def exchange(x, axes):
    return lax.all_to_all(x, axes, split_axis=0, concat_axis=0, tiled=True)


def on_device(positions, spacing, crossings, target, first_weight, head_weight):
    own = jnp.concatenate(
        [first_weight[0].astype(f32).T, head_weight[0].astype(f32)], axis=0
    )
    weights = [own] + [with_member(own, difference) for difference in range(1, GROUP)]
    bricks = GROUP * PEERS
    own_place = jnp.stack([lax.axis_index("gz"), lax.axis_index(PEER_AXES)]).astype(jnp.int32)
    send, index, dest = pack(own_place, positions, spacing.T, crossings.T)
    target_rows = jnp.pad(target.T, ((0, 0), (0, 125)))
    received = exchange(send, PEER_AXES)
    small, saved, steps, used = forward(received, weights)
    grads, rendered = ray_level(exchange(small, PEER_AXES), index, dest, target_rows)
    grads = exchange(grads, PEER_AXES)
    upstream, *far = backward_far(grads, saved, steps, received, used, weights[HALF:])
    near = backward_near(upstream, received, used, weights[:HALF])
    arrived = [near[0]]
    arrived += [with_member(far[i], HALF + i) for i in range(HALF)]
    arrived += [with_member(near[i], i) for i in range(1, HALF)]
    total, square = add_up(arrived, bricks)
    squares = exchange(square, ALL)
    first_update, head_update = normalize(total, squares, bricks * (64 * HIDDEN))
    return (rendered, first_update, head_update)


def solution(mesh):
    in_specs = (
        P(None, ALL, None),
        P(ALL, None),
        P(ALL, None),
        P(None, ALL),
        P(ALL, None, None),
        P(ALL, None, None),
    )
    out_specs = (P(None, ALL), P(ALL, None, None), P(ALL, None, None))
    return jax.shard_map(
        on_device, mesh=mesh, in_specs=in_specs, out_specs=out_specs, check_vma=False
    )
```

```python
import jax
import jax.numpy as jnp
from jax import lax
from jax.experimental import pallas as pl
from jax.experimental.pallas import tpu as pltpu
from jax.sharding import PartitionSpec as P

FREQS = 10
SAMPLES = 64
SEGS = 8
CAP = 3
ANCHOR = 5
NORM_EPS = 1e-06

RAYS = 48
GROUP = 8
PEERS = 32
SLOTS = GROUP * CAP
PAIRS = SLOTS // 2
ROWS = PEERS // 2
PITCH = ROWS + 1
TILE = PEERS * SAMPLES
ENTRIES = RAYS * SEGS
LIST = SLOTS + 2
STEP_ROW = 3 * PAIRS
WIRE = STEP_ROW + 1
HIDDEN = 256
FORWARD_CHUNK = 2048
BACKWARD_CHUNK = 512
VMEM = 56 * 1024 * 1024
SOME_VMEM = 24 * 1024 * 1024
ALL = ("gx", "gy", "gz")
PEER_AXES = ("gx", "gy")
GROUP_AXIS = "gz"

SIN_TERMS = (
    6.283185160116253,
    -41.34165503574907,
    81.60100428250003,
    -76.54978619700827,
    39.536730859838705,
)

f32 = jnp.float32
bf16 = jnp.bfloat16


def iota(shape, dim):
    return lax.broadcasted_iota(jnp.int32, shape, dim)


def nt_dot(a, b, precision=None):
    return lax.dot_general(
        a, b, (((1,), (1,)), ((), ())), preferred_element_type=f32, precision=precision
    )


def tn_dot(a, b):
    return lax.dot_general(a, b, (((0,), (0,)), ((), ())), preferred_element_type=f32)


def matrix_cost(tile_passes):
    return pl.CostEstimate(
        flops=tile_passes * 2 * HIDDEN * HIDDEN * TILE, bytes_accessed=4 << 20, transcendentals=0
    )


def wire_row(row):
    return pl.ds(128 * row if isinstance(row, int) else pl.multiple_of(128 * row, 128), 128)


def split3(x):
    high = x.astype(bf16)
    rest = x - high.astype(f32)
    mid = rest.astype(bf16)
    return high, mid, (rest - mid.astype(f32)).astype(bf16)


def pick(one_hot, x):
    high, mid, low = split3(x)
    total = jnp.dot(one_hot, low, preferred_element_type=f32)
    total += jnp.dot(one_hot, mid, preferred_element_type=f32)
    return total + jnp.dot(one_hot, high, preferred_element_type=f32)


def add_lanes(x, mask):
    ones = as_matrix(mask).astype(bf16)
    high, mid, low = split3(x)
    total = jnp.dot(low, ones, preferred_element_type=f32)
    total += jnp.dot(mid, ones, preferred_element_type=f32)
    return total + jnp.dot(high, ones, preferred_element_type=f32)


def column_of(rows_ref):
    rows = rows_ref[...].astype(f32)
    padded = jnp.concatenate([rows, jnp.zeros((SEGS, 128 - RAYS), f32)], axis=1).T
    return jnp.concatenate([padded[:RAYS, s : s + 1] for s in range(SEGS)], axis=0)


def pack_kernel(
    member_ref, peer_ref, pos_ref, step_ref, cross_ref, send_ref, index_ref, dest_ref, data_ref
):
    brick_col = column_of(cross_ref)
    step_col = column_of(step_ref)
    sub = iota((ENTRIES, ENTRIES), 0)
    lane = iota((ENTRIES, ENTRIES), 1)
    brick_row = jnp.sum(jnp.where(sub == lane, brick_col, 0.0), axis=0, keepdims=True)
    same = brick_col == brick_row
    rank_col = jnp.sum(jnp.where(same & (lane < sub), 1.0, 0.0), axis=1, keepdims=True)
    rank_row = jnp.sum(jnp.where(same & (sub < lane), 1.0, 0.0), axis=0, keepdims=True)
    own = member_ref[0].astype(f32)

    def place(number, rank):
        dest = jnp.floor(number * (1.0 / GROUP))
        ahead = number - GROUP * dest - own
        ahead = jnp.where(ahead < 0.0, ahead + GROUP, ahead)
        return dest, ahead * CAP + rank

    dest_col, slot_col = place(brick_col, rank_col)
    dest_row, slot_row = place(brick_row, rank_row)
    pair_row = jnp.floor(slot_row * 0.5)
    half_row = slot_row - 2.0 * pair_row
    half_row = jnp.where(peer_ref[0] < ROWS, half_row, 1.0 - half_row)
    target_row = pair_row * PEERS + dest_row
    here = sub.astype(f32) == target_row
    one_hot = jnp.concatenate(
        [jnp.where(here & (half_row == half), 1.0, 0.0).astype(bf16) for half in (0.0, 1.0)], axis=1
    )
    left = iota((RAYS, 128), 1) < SAMPLES
    for c in range(3):
        for q in range(SEGS // 2):
            x = pos_ref[c, :, 128 * q : 128 * q + 128]
            y = pltpu.roll(x, SAMPLES, 1)
            blocks = (
                (0, 2 * q, jnp.where(left, x, 0.0)),
                (0, 2 * q + 1, jnp.where(left, y, 0.0)),
                (1, 2 * q, jnp.where(left, 0.0, y)),
                (1, 2 * q + 1, jnp.where(left, 0.0, x)),
            )
            for half, s, block in blocks:
                row = half * ENTRIES + s * RAYS
                for part, value in enumerate(split3(block)):
                    data_ref[part, row : row + RAYS, 128 * c : 128 * c + 128] = value
    total = jnp.dot(one_hot, data_ref[2], preferred_element_type=f32)
    total += jnp.dot(one_hot, data_ref[1], preferred_element_type=f32)
    total += jnp.dot(one_hot, data_ref[0], preferred_element_type=f32)
    for pair in range(PAIRS):
        for c in range(3):
            send_ref[:, 0, wire_row(3 * pair + c)] = total[
                pair * PEERS : (pair + 1) * PEERS, 128 * c : 128 * c + 128
            ]
    to_dest = jnp.where(iota((PEERS, ENTRIES), 0).astype(f32) == dest_row, 1.0, 0.0)
    lane_128 = iota((ENTRIES, 128), 1)
    by_slot = jnp.where(lane_128.astype(f32) == slot_col, step_col, 0.0)
    send_ref[:, 0, wire_row(STEP_ROW)] = pick(to_dest.astype(bf16), by_slot)
    index_ref[...] = jnp.where(lane_128 < 64, dest_col, slot_col)
    dest_ref[...] = jnp.broadcast_to(dest_row, (8, ENTRIES))


def pack(member, peer, positions, spacing, crossings):
    vmem = pl.BlockSpec(memory_space=pltpu.VMEM)
    smem = pl.BlockSpec(memory_space=pltpu.SMEM)
    return pl.pallas_call(
        pack_kernel,
        out_shape=(
            jax.ShapeDtypeStruct((PEERS, 1, 128 * WIRE), f32),
            jax.ShapeDtypeStruct((ENTRIES, 128), f32),
            jax.ShapeDtypeStruct((8, ENTRIES), f32),
        ),
        in_specs=[smem, smem, vmem, vmem, vmem],
        out_specs=(vmem, vmem, vmem),
        scratch_shapes=[pltpu.VMEM((3, 2 * ENTRIES, 384), bf16)],
        compiler_params=pltpu.CompilerParams(vmem_limit_bytes=VMEM),
        name="pack",
    )(member, peer, positions, spacing, crossings)


def sine_of_turns(y):
    z = y * y
    value = SIN_TERMS[-1]
    for term in SIN_TERMS[-2::-1]:
        value = value * z + term
    return value * y


def put_row(wave_ref, row, values):
    wave_ref[row * PITCH : row * PITCH + ROWS, :] = values


def encode_into(enc_ref, kept_ref, wave_ref, recv_ref, slot):
    pair = slot // 2
    near_side = (iota((ROWS, 128), 1) < SAMPLES) == (slot == 2 * pair)
    points = jnp.concatenate(
        [
            jnp.where(
                near_side,
                recv_ref[:ROWS, 0, wire_row(3 * pair + c)],
                recv_ref[ROWS:, 0, wire_row(3 * pair + c)],
            )
            for c in range(3)
        ],
        axis=0,
    )
    for k in range(FREQS):
        if k % ANCHOR == 0:
            turns = points * (0.5 * 2.0**k)
            turns = turns - jnp.round(turns)
            size = jnp.abs(turns)
            cosine = sine_of_turns(0.25 - size)
            sine = sine_of_turns(jnp.minimum(size, 0.5 - size))
            sine = jnp.where(turns < 0.0, -sine, sine)
        else:
            square = sine * sine
            sine = sine * cosine
            sine = sine + sine
            cosine = 1.0 - (square + square)
        for c in range(3):
            put_row(wave_ref, 6 * k + c, sine[c * ROWS : (c + 1) * ROWS])
            put_row(wave_ref, 6 * k + 3 + c, cosine[c * ROWS : (c + 1) * ROWS])
    for r in range(ROWS):
        lanes = slice(128 * r, 128 * r + 128)
        waves = wave_ref[pl.ds(r, 64, stride=PITCH), :].astype(bf16)
        enc_ref[:, lanes] = waves
        kept_ref[slot, :, lanes] = waves


def in_turns(used_ref, count, prepare, work, buffers):
    here, other = buffers
    prepare(here, used_ref[0])

    def turn(number, carry):
        place = 2 * number
        prepare(other, used_ref[place + 1])
        work(here, used_ref[place])

        @pl.when(place + 1 < count)
        def _():
            prepare(here, used_ref[place + 2])
            work(other, used_ref[place + 1])

        return carry

    lax.fori_loop(0, (count + 1) // 2, turn, 0)


def spread(near, far, slot, lane_index):
    near_side = (iota((ROWS, 128), 1) < SAMPLES) == (slot % 2 == 0)
    return jnp.where(
        near_side, near[:, lane_index : lane_index + 1], far[:, lane_index : lane_index + 1]
    )


def same_half():
    i = iota((128, 128), 0)
    j = iota((128, 128), 1)
    return i, j, (i < SAMPLES) == (j < SAMPLES)


def as_matrix(mask):
    return jnp.where(mask, 1.0, 0.0)


def forward_kernel(*refs):
    recv_ref = refs[0]
    weight_refs = refs[1 : 1 + GROUP]
    small_ref, saved_ref, step_ref, kept_ref, used_ref = refs[1 + GROUP : 6 + GROUP]
    w_ref, head_ref, enc_ref, next_ref, wave_ref, out_ref = refs[6 + GROUP :]

    for i in range(GROUP):
        packed = weight_refs[i][...]
        w_ref[i] = (0.5 * packed).T.astype(bf16)
        head_ref[i] = packed[48:64].astype(bf16)

    near = recv_ref[:ROWS, 0, wire_row(STEP_ROW)]
    far = recv_ref[ROWS:, 0, wire_row(STEP_ROW)]
    most = jnp.max(jnp.maximum(near, far), axis=0, keepdims=True)
    count = jnp.int32(0)
    for place in range(LIST):
        used_ref[place] = 0
    for slot in range(SLOTS):
        used_ref[count] = slot
        count += (most[0, slot] > 0.0).astype(jnp.int32)
    used_ref[LIST] = count
    lane = iota((ROWS, 128), 1)
    turned = pltpu.roll(far, SAMPLES, 1)
    chosen = [
        jnp.where(lane == slot, near, jnp.where(lane == slot + SAMPLES, turned, 0.0))
        for slot in range(SLOTS)
    ]
    i, j, same = same_half()
    steps = add_lanes(jnp.concatenate(chosen, axis=0), same == (i % 2 == 0))
    step_ref[...] = steps.reshape(SLOTS, ROWS, 128)
    out_ref[...] = jnp.zeros((4, SLOTS, ROWS, 128), f32)

    def network(enc_ref, slot):
        first = w_ref[slot // CAP]
        head = head_ref[slot // CAP]
        for n in range(TILE // FORWARD_CHUNK):
            encoded = enc_ref[:, n * FORWARD_CHUNK : (n + 1) * FORWARD_CHUNK]
            half = jnp.dot(first, encoded, preferred_element_type=f32)
            hidden = (half + half * jnp.tanh(half)).astype(bf16)
            output = jnp.dot(head, hidden, preferred_element_type=f32)
            for r in range(FORWARD_CHUNK // 128):
                row = n * (FORWARD_CHUNK // 128) + r
                for v in range(4):
                    out_ref[v, slot, row : row + 1, :] = output[
                        12 + v : 13 + v, 128 * r : 128 * r + 128
                    ]

    wave_ref[...] = jnp.zeros(wave_ref.shape, f32)

    def prepare(ref, slot):
        encode_into(ref, kept_ref, wave_ref, recv_ref, slot)

    in_turns(used_ref, count, prepare, network, (enc_ref, next_ref))

    rows = SLOTS * ROWS
    outputs = [out_ref[v].reshape(rows, 128) for v in range(4)]
    raw = outputs[0]
    density = jnp.maximum(raw, 0.0) + jnp.log1p(jnp.exp(-jnp.abs(raw)))
    optical = density * steps
    inclusive = add_lanes(optical, same & (i <= j))
    leaving = jnp.exp(-inclusive)
    weight = jnp.exp(optical - inclusive) - leaving
    saved_ref[3] = jax.nn.sigmoid(raw).reshape(SLOTS, ROWS, 128)
    saved_ref[4] = weight.reshape(SLOTS, ROWS, 128)
    saved_ref[5] = leaving.reshape(SLOTS, ROWS, 128)
    i = iota((128, 256), 0)
    first_half = iota((128, 256), 1) < 128
    results = []
    for v in range(3):
        colour = jax.nn.sigmoid(outputs[1 + v])
        saved_ref[v] = colour.reshape(SLOTS, ROWS, 128)
        results.append(add_lanes(weight * colour, (i < SAMPLES) == first_half))
    results.append(add_lanes(leaving, i == jnp.where(first_half, SAMPLES - 1, 127)))
    for side in range(2):
        gathered = jnp.zeros((ROWS, 128), f32)
        for v in range(4):
            for slot in range(SLOTS):
                half = (side + slot) % 2
                block = results[v][slot * ROWS : (slot + 1) * ROWS, 128 * half : 128 * half + 128]
                gathered = jnp.where(lane == v * SLOTS + slot, block, gathered)
        small_ref[side * ROWS : (side + 1) * ROWS, :] = gathered


def forward(received, weights):
    vmem = pl.BlockSpec(memory_space=pltpu.VMEM)
    smem = pl.BlockSpec(memory_space=pltpu.SMEM)
    return pl.pallas_call(
        forward_kernel,
        out_shape=(
            jax.ShapeDtypeStruct((PEERS, 128), f32),
            jax.ShapeDtypeStruct((6, SLOTS, ROWS, 128), f32),
            jax.ShapeDtypeStruct((SLOTS, ROWS, 128), f32),
            jax.ShapeDtypeStruct((SLOTS, 64, TILE), bf16),
            jax.ShapeDtypeStruct((LIST + 1,), jnp.int32),
        ),
        in_specs=[vmem] * (1 + GROUP),
        out_specs=(vmem, vmem, vmem, vmem, smem),
        scratch_shapes=[
            pltpu.VMEM((GROUP, HIDDEN, 64), bf16),
            pltpu.VMEM((GROUP, 16, HIDDEN), bf16),
            pltpu.VMEM((64, TILE), bf16),
            pltpu.VMEM((64, TILE), bf16),
            pltpu.VMEM((64 * PITCH, 128), f32),
            pltpu.VMEM((4, SLOTS, ROWS, 128), f32),
        ],
        compiler_params=pltpu.CompilerParams(vmem_limit_bytes=SOME_VMEM),
        cost_estimate=matrix_cost(SLOTS * 2),
        name="forward",
    )(received, *weights)


def ray_kernel(small_ref, index_ref, dest_ref, target_ref, grads_ref, rendered_ref):
    lane = iota((ENTRIES, 128), 1)
    value = lane // SLOTS
    slot = (lane - value * SLOTS).astype(f32)
    dest_col = index_ref[:, 0:1]
    slot_col = index_ref[:, 64:65]
    to_entry = jnp.where(lane.astype(f32) == dest_col, 1.0, 0.0).astype(bf16)
    small = jnp.concatenate([small_ref[...], jnp.zeros((128 - PEERS, 128), f32)], axis=0)
    mine = (slot == slot_col) & (value < 4)
    found = jnp.where(mine, pick(to_entry, small), 0.0)
    i = iota((128, 128), 0)
    j = iota((128, 128), 1)
    segments = add_lanes(found, (i // SLOTS == j) & (j < 4))

    lane = iota((RAYS, 128), 1)
    parts = [segments[s * RAYS : (s + 1) * RAYS] for s in range(SEGS)]
    trans = [jnp.broadcast_to(part[:, 3:4], (RAYS, 128)) for part in parts]
    prefix = [jnp.ones((RAYS, 128), f32)]
    for s in range(SEGS - 1):
        prefix.append(prefix[s] * trans[s])
    rendered = prefix[0] * parts[0]
    for s in range(1, SEGS):
        rendered += prefix[s] * parts[s]
    target = jnp.concatenate([target_ref[...], jnp.zeros((3, 128 - RAYS), f32)], axis=1)
    target = jnp.concatenate([target, jnp.zeros((125, 128), f32)], axis=0).T[:RAYS]
    residual = jnp.where(lane < 3, rendered - target, 0.0)
    behind = jnp.zeros((RAYS, 128), f32)
    grads = [None] * SEGS
    for s in range(SEGS - 1, -1, -1):
        through = prefix[s] * jnp.sum(behind * residual, axis=1, keepdims=True)
        grads[s] = jnp.where(lane == 3, through, prefix[s] * residual)
        behind = parts[s] + trans[s] * behind
    spread_back = add_lanes(jnp.concatenate(grads, axis=0), (j // SLOTS == i) & (i < 4))
    to_dest = jnp.where(iota((PEERS, ENTRIES), 0).astype(f32) == dest_ref[0:1, :], 1.0, 0.0)
    grads_ref[...] = pick(to_dest.astype(bf16), jnp.where(mine, spread_back, 0.0))
    eye = as_matrix(iota((8, 128), 0) == iota((8, 128), 1))
    rendered_ref[...] = nt_dot(eye, rendered, lax.Precision.HIGHEST)[0:3]


def ray_level(small, index, dest, target):
    return pl.pallas_call(
        ray_kernel,
        out_shape=(
            jax.ShapeDtypeStruct((PEERS, 128), f32),
            jax.ShapeDtypeStruct((3, RAYS), f32),
        ),
        compiler_params=pltpu.CompilerParams(vmem_limit_bytes=SOME_VMEM),
        name="rays",
    )(small, index, dest, target)


def upstream_into(up_ref, grads_ref, saved_ref, step_ref):
    near = grads_ref[:ROWS]
    far = grads_ref[ROWS:]
    for v in range(4):
        for slot in range(SLOTS):
            up_ref[v, slot] = spread(near, far, slot, v * SLOTS + slot)

    rows = SLOTS * ROWS

    def flat(x):
        return x.reshape(rows, 128)

    i, j, same = same_half()
    weight = flat(saved_ref[4])
    leaving = flat(saved_ref[5])
    shading = flat(saved_ref[0]) * flat(up_ref[0])
    shading += flat(saved_ref[1]) * flat(up_ref[1])
    shading += flat(saved_ref[2]) * flat(up_ref[2])
    after = add_lanes(weight * shading, same & (i > j))
    last = add_lanes(leaving, same & ((i == SAMPLES - 1) | (i == 127)))
    grad_depth = shading * leaving - after - flat(up_ref[3]) * last
    upstream = [grad_depth * flat(step_ref[...]) * flat(saved_ref[3])]
    for v in range(3):
        colour = flat(saved_ref[v])
        upstream.append(weight * flat(up_ref[v]) * colour * (1.0 - colour))
    for v in range(4):
        up_ref[v] = upstream[v].reshape(SLOTS, ROWS, 128)


def backward_kernel(*refs):
    member_ref, grads_ref, saved_ref, step_ref, kept_ref, used_ref = refs[:6]
    weight_refs = refs[6 : 6 + GROUP]
    total_ref, up_ref, both_ref, sum_ref, input_ref, next_ref, wave_ref, right_ref = refs[
        6 + GROUP :
    ]
    both_ref[...] = jnp.zeros(both_ref.shape, bf16)
    for i in range(GROUP):
        packed = (0.5 * weight_refs[i][...]).astype(bf16)
        both_ref[i, :64, :HIDDEN] = packed
        both_ref[i, 64:, HIDDEN:] = packed[48:]
    sum_ref[...] = jnp.zeros(sum_ref.shape, f32)
    upstream_into(up_ref, grads_ref, saved_ref, step_ref)
    wave_ref[...] = jnp.zeros(wave_ref.shape, f32)

    def prepare(ref, slot):
        for v in range(4):
            put_row(wave_ref, 12 + v, up_ref[v, slot])
        for r in range(ROWS):
            ref[:, 128 * r : 128 * r + 128] = wave_ref[pl.ds(r, 16, stride=PITCH), :].astype(bf16)

    def work(ref, slot):
        brick = slot // CAP
        both = both_ref[brick]
        for n in range(TILE // BACKWARD_CHUNK):
            chunk = slice(n * BACKWARD_CHUNK, (n + 1) * BACKWARD_CHUNK)
            given = jnp.concatenate([kept_ref[slot, :, chunk], ref[:, chunk]], axis=0)
            product = tn_dot(given, both)
            half = product[:, :HIDDEN]
            bend = jnp.tanh(half)
            bent = half * bend
            slope = (1.0 + bend) * ((1.0 + half) - bent)
            right_ref[chunk, HIDDEN:] = (half + bent).astype(bf16)
            right_ref[chunk, :HIDDEN] = (product[:, HIDDEN:] * slope).astype(bf16)
        given = jnp.concatenate([kept_ref[slot], ref[...]], axis=0)
        sum_ref[brick] += jnp.dot(given, right_ref[...], preferred_element_type=f32)

    in_turns(used_ref, used_ref[LIST], prepare, work, (input_ref, next_ref))
    for i in range(GROUP):
        member = lax.rem(member_ref[0] + i, GROUP)
        total_ref[member, :48] = sum_ref[i, :48, :HIDDEN]
        total_ref[member, 48:] = sum_ref[i, 48:64, :HIDDEN] + sum_ref[i, 64:, HIDDEN:]


def backward(member, grads, saved, steps, kept, used, weights):
    vmem = pl.BlockSpec(memory_space=pltpu.VMEM)
    smem = pl.BlockSpec(memory_space=pltpu.SMEM)
    return pl.pallas_call(
        backward_kernel,
        out_shape=jax.ShapeDtypeStruct((GROUP, 64, HIDDEN), f32),
        in_specs=[smem, vmem, vmem, vmem, vmem, smem] + [vmem] * GROUP,
        out_specs=vmem,
        scratch_shapes=[
            pltpu.VMEM((4, SLOTS, ROWS, 128), f32),
            pltpu.VMEM((GROUP, 80, 2 * HIDDEN), bf16),
            pltpu.VMEM((GROUP, 80, 2 * HIDDEN), f32),
            pltpu.VMEM((16, TILE), bf16),
            pltpu.VMEM((16, TILE), bf16),
            pltpu.VMEM((16 * PITCH, 128), f32),
            pltpu.VMEM((TILE, 2 * HIDDEN), bf16),
        ],
        compiler_params=pltpu.CompilerParams(vmem_limit_bytes=SOME_VMEM),
        cost_estimate=matrix_cost(SLOTS * 4),
        name="backward",
    )(member, grads, saved, steps, kept, used, *weights)


def sum_kernel(*refs):
    parts_ref, total_ref, square_ref = refs
    total = parts_ref[0]
    for i in range(1, GROUP):
        total += parts_ref[i]
    total_ref[...] = total
    square = jnp.sum(jnp.sum(total * total, axis=1, keepdims=True), axis=0, keepdims=True)
    square_ref[...] = jnp.broadcast_to(square, square_ref.shape)


def add_up(partials, bricks):
    return pl.pallas_call(
        sum_kernel,
        out_shape=(
            jax.ShapeDtypeStruct((64, HIDDEN), f32),
            jax.ShapeDtypeStruct((bricks, 128), f32),
        ),
        compiler_params=pltpu.CompilerParams(vmem_limit_bytes=SOME_VMEM),
        name="add_up",
    )(partials)


def normalize(total, squares, count):
    def body(total_ref, squares_ref, first_ref, head_ref):
        overall = jnp.sum(squares_ref[:, 0:1], axis=0, keepdims=True)
        scaled = total_ref[...] * lax.rsqrt(overall / count + NORM_EPS)
        first_ref[:, 0, :] = scaled[: 6 * FREQS]
        head_ref[0] = scaled[6 * FREQS :]

    first, head = pl.pallas_call(
        body,
        out_shape=(
            jax.ShapeDtypeStruct((6 * FREQS, 1, HIDDEN), f32),
            jax.ShapeDtypeStruct((1, 4, HIDDEN), f32),
        ),
        compiler_params=pltpu.CompilerParams(vmem_limit_bytes=SOME_VMEM),
        name="normalize",
    )(total, squares)
    return first.transpose(1, 2, 0), head


def from_ahead(x, distance):
    return lax.ppermute(x, GROUP_AXIS, [(i, (i - distance) % GROUP) for i in range(GROUP)])


def exchange(x, axes):
    return lax.all_to_all(x, axes, split_axis=0, concat_axis=0, tiled=True)


def on_device(positions, spacing, crossings, target, first_weight, head_weight):
    own = jnp.concatenate(
        [first_weight[0].astype(f32).T, head_weight[0].astype(f32)], axis=0
    )
    weights = [own] + [from_ahead(own, distance) for distance in range(1, GROUP)]
    bricks = GROUP * PEERS
    member = lax.axis_index(GROUP_AXIS).astype(jnp.int32).reshape(1)
    peer = lax.axis_index(PEER_AXES).astype(jnp.int32).reshape(1)
    send, index, dest = pack(member, peer, positions, spacing.T, crossings.T)
    received = exchange(send, PEER_AXES)
    small, saved, steps, kept, used = forward(received, weights)
    grads, rendered = ray_level(exchange(small, PEER_AXES), index, dest, target)
    grads = exchange(grads, PEER_AXES)
    partials = backward(member, grads, saved, steps, kept, used, weights)
    total, square = add_up(exchange(partials, GROUP_AXIS), bricks)
    squares = exchange(square, ALL)
    first_update, head_update = normalize(total, squares, bricks * (64 * HIDDEN))
    return (rendered, first_update, head_update)


def solution(mesh):
    in_specs = (
        P(None, ALL, None),
        P(ALL, None),
        P(ALL, None),
        P(None, ALL),
        P(ALL, None, None),
        P(ALL, None, None),
    )
    out_specs = (P(None, ALL), P(ALL, None, None), P(ALL, None, None))
    return jax.shard_map(
        on_device, mesh=mesh, in_specs=in_specs, out_specs=out_specs, check_vma=False
    )
```

```python
import jax
import jax.numpy as jnp
from jax import lax
from jax.experimental import pallas as pl
from jax.experimental.pallas import tpu as pltpu
from jax.sharding import PartitionSpec as P

FREQS = 10
SAMPLES = 64
SEGS = 8
CAP = 3
ANCHOR = 5
NORM_EPS = 1e-06

RAYS = 48
GROUP = 8
PEERS = 32
SLOTS = GROUP * CAP
PAIRS = SLOTS // 2
ROWS = PEERS // 2
PITCH = ROWS + 1
TILE = PEERS * SAMPLES
ENTRIES = RAYS * SEGS
LIST = SLOTS + 2
STEP_ROW = 3 * PAIRS
WIRE = STEP_ROW + 1
HIDDEN = 256
FORWARD_CHUNK = 2048
BACKWARD_CHUNK = 512
VMEM = 56 * 1024 * 1024
SOME_VMEM = 24 * 1024 * 1024
ALL = ("gx", "gy", "gz")
PEER_AXES = ("gx", "gy")
GROUP_AXIS = "gz"

SIN_TERMS = (
    6.283185160116253,
    -41.34165503574907,
    81.60100428250003,
    -76.54978619700827,
    39.536730859838705,
)

f32 = jnp.float32
bf16 = jnp.bfloat16


def iota(shape, dim):
    return lax.broadcasted_iota(jnp.int32, shape, dim)


def nt_dot(a, b, precision=None):
    return lax.dot_general(
        a, b, (((1,), (1,)), ((), ())), preferred_element_type=f32, precision=precision
    )


def tn_dot(a, b):
    return lax.dot_general(a, b, (((0,), (0,)), ((), ())), preferred_element_type=f32)


def matrix_cost(tile_passes):
    return pl.CostEstimate(
        flops=tile_passes * 2 * HIDDEN * HIDDEN * TILE, bytes_accessed=4 << 20, transcendentals=0
    )


def wire_row(row):
    return pl.ds(128 * row if isinstance(row, int) else pl.multiple_of(128 * row, 128), 128)


def split3(x):
    high = x.astype(bf16)
    rest = x - high.astype(f32)
    mid = rest.astype(bf16)
    return high, mid, (rest - mid.astype(f32)).astype(bf16)


def pick(one_hot, x):
    high, mid, low = split3(x)
    total = jnp.dot(one_hot, low, preferred_element_type=f32)
    total += jnp.dot(one_hot, mid, preferred_element_type=f32)
    return total + jnp.dot(one_hot, high, preferred_element_type=f32)


def add_lanes(x, mask):
    ones = as_matrix(mask).astype(bf16)
    high, mid, low = split3(x)
    total = jnp.dot(low, ones, preferred_element_type=f32)
    total += jnp.dot(mid, ones, preferred_element_type=f32)
    return total + jnp.dot(high, ones, preferred_element_type=f32)


def column_of(rows_ref):
    rows = rows_ref[...].astype(f32)
    padded = jnp.concatenate([rows, jnp.zeros((SEGS, 128 - RAYS), f32)], axis=1).T
    return jnp.concatenate([padded[:RAYS, s : s + 1] for s in range(SEGS)], axis=0)


def pack_kernel(
    member_ref, peer_ref, pos_ref, step_ref, cross_ref, send_ref, index_ref, dest_ref, data_ref
):
    brick_col = column_of(cross_ref)
    step_col = column_of(step_ref)
    sub = iota((ENTRIES, ENTRIES), 0)
    lane = iota((ENTRIES, ENTRIES), 1)
    brick_row = jnp.sum(jnp.where(sub == lane, brick_col, 0.0), axis=0, keepdims=True)
    same = brick_col == brick_row
    rank_col = jnp.sum(jnp.where(same & (lane < sub), 1.0, 0.0), axis=1, keepdims=True)
    rank_row = jnp.sum(jnp.where(same & (sub < lane), 1.0, 0.0), axis=0, keepdims=True)
    own = member_ref[0].astype(f32)

    def place(number, rank):
        dest = jnp.floor(number * (1.0 / GROUP))
        ahead = number - GROUP * dest - own
        ahead = jnp.where(ahead < 0.0, ahead + GROUP, ahead)
        return dest, ahead * CAP + rank

    dest_col, slot_col = place(brick_col, rank_col)
    dest_row, slot_row = place(brick_row, rank_row)
    pair_row = jnp.floor(slot_row * 0.5)
    half_row = slot_row - 2.0 * pair_row
    half_row = jnp.where(peer_ref[0] < ROWS, half_row, 1.0 - half_row)
    target_row = pair_row * PEERS + dest_row
    here = sub.astype(f32) == target_row
    one_hot = jnp.concatenate(
        [jnp.where(here & (half_row == half), 1.0, 0.0).astype(bf16) for half in (0.0, 1.0)], axis=1
    )
    left = iota((RAYS, 128), 1) < SAMPLES
    for c in range(3):
        for q in range(SEGS // 2):
            x = pos_ref[c, :, 128 * q : 128 * q + 128]
            y = pltpu.roll(x, SAMPLES, 1)
            blocks = (
                (0, 2 * q, jnp.where(left, x, 0.0)),
                (0, 2 * q + 1, jnp.where(left, y, 0.0)),
                (1, 2 * q, jnp.where(left, 0.0, y)),
                (1, 2 * q + 1, jnp.where(left, 0.0, x)),
            )
            for half, s, block in blocks:
                row = half * ENTRIES + s * RAYS
                for part, value in enumerate(split3(block)):
                    data_ref[part, row : row + RAYS, 128 * c : 128 * c + 128] = value
    total = jnp.dot(one_hot, data_ref[2], preferred_element_type=f32)
    total += jnp.dot(one_hot, data_ref[1], preferred_element_type=f32)
    total += jnp.dot(one_hot, data_ref[0], preferred_element_type=f32)
    for pair in range(PAIRS):
        for c in range(3):
            send_ref[:, 0, wire_row(3 * pair + c)] = total[
                pair * PEERS : (pair + 1) * PEERS, 128 * c : 128 * c + 128
            ]
    to_dest = jnp.where(iota((PEERS, ENTRIES), 0).astype(f32) == dest_row, 1.0, 0.0)
    lane_128 = iota((ENTRIES, 128), 1)
    by_slot = jnp.where(lane_128.astype(f32) == slot_col, step_col, 0.0)
    send_ref[:, 0, wire_row(STEP_ROW)] = pick(to_dest.astype(bf16), by_slot)
    index_ref[...] = jnp.where(lane_128 < 64, dest_col, slot_col)
    dest_ref[...] = jnp.broadcast_to(dest_row, (8, ENTRIES))


def pack(member, peer, positions, spacing, crossings):
    vmem = pl.BlockSpec(memory_space=pltpu.VMEM)
    smem = pl.BlockSpec(memory_space=pltpu.SMEM)
    return pl.pallas_call(
        pack_kernel,
        out_shape=(
            jax.ShapeDtypeStruct((PEERS, 1, 128 * WIRE), f32),
            jax.ShapeDtypeStruct((ENTRIES, 128), f32),
            jax.ShapeDtypeStruct((8, ENTRIES), f32),
        ),
        in_specs=[smem, smem, vmem, vmem, vmem],
        out_specs=(vmem, vmem, vmem),
        scratch_shapes=[pltpu.VMEM((3, 2 * ENTRIES, 384), bf16)],
        compiler_params=pltpu.CompilerParams(vmem_limit_bytes=VMEM),
        name="pack",
    )(member, peer, positions, spacing, crossings)


def sine_of_turns(y):
    z = y * y
    value = SIN_TERMS[-1]
    for term in SIN_TERMS[-2::-1]:
        value = value * z + term
    return value * y


def put_row(wave_ref, row, values):
    wave_ref[row * PITCH : row * PITCH + ROWS, :] = values


def encode_into(enc_ref, kept_ref, wave_ref, recv_ref, slot):
    pair = slot // 2
    near_side = (iota((ROWS, 128), 1) < SAMPLES) == (slot == 2 * pair)
    points = jnp.concatenate(
        [
            jnp.where(
                near_side,
                recv_ref[:ROWS, 0, wire_row(3 * pair + c)],
                recv_ref[ROWS:, 0, wire_row(3 * pair + c)],
            )
            for c in range(3)
        ],
        axis=0,
    )
    for k in range(FREQS):
        if k % ANCHOR == 0:
            turns = points * (0.5 * 2.0**k)
            turns = turns - jnp.round(turns)
            size = jnp.abs(turns)
            cosine = sine_of_turns(0.25 - size)
            sine = sine_of_turns(jnp.minimum(size, 0.5 - size))
            sine = jnp.where(turns < 0.0, -sine, sine)
        else:
            square = sine * sine
            sine = sine * cosine
            sine = sine + sine
            cosine = 1.0 - (square + square)
        for c in range(3):
            put_row(wave_ref, 6 * k + c, sine[c * ROWS : (c + 1) * ROWS])
            put_row(wave_ref, 6 * k + 3 + c, cosine[c * ROWS : (c + 1) * ROWS])
    for r in range(ROWS):
        lanes = slice(128 * r, 128 * r + 128)
        waves = wave_ref[pl.ds(r, 64, stride=PITCH), :].astype(bf16)
        enc_ref[:, lanes] = waves
        kept_ref[slot, :, lanes] = waves


def in_turns(used_ref, count, prepare, work, buffers):
    here, other = buffers
    prepare(here, used_ref[0])

    def turn(number, carry):
        place = 2 * number
        prepare(other, used_ref[place + 1])
        work(here, used_ref[place])

        @pl.when(place + 1 < count)
        def _():
            prepare(here, used_ref[place + 2])
            work(other, used_ref[place + 1])

        return carry

    lax.fori_loop(0, (count + 1) // 2, turn, 0)


def spread(near, far, slot, lane_index):
    near_side = (iota((ROWS, 128), 1) < SAMPLES) == (slot % 2 == 0)
    return jnp.where(
        near_side, near[:, lane_index : lane_index + 1], far[:, lane_index : lane_index + 1]
    )


def same_half():
    i = iota((128, 128), 0)
    j = iota((128, 128), 1)
    return i, j, (i < SAMPLES) == (j < SAMPLES)


def as_matrix(mask):
    return jnp.where(mask, 1.0, 0.0)


def forward_kernel(*refs):
    recv_ref = refs[0]
    weight_refs = refs[1 : 1 + GROUP]
    small_ref, saved_ref, step_ref, kept_ref, used_ref = refs[1 + GROUP : 6 + GROUP]
    w_ref, head_ref, enc_ref, next_ref, wave_ref, out_ref = refs[6 + GROUP :]

    for i in range(GROUP):
        packed = weight_refs[i][...]
        w_ref[i] = (0.5 * packed).T.astype(bf16)
        head_ref[i] = packed[48:64].astype(bf16)

    near = recv_ref[:ROWS, 0, wire_row(STEP_ROW)]
    far = recv_ref[ROWS:, 0, wire_row(STEP_ROW)]
    most = jnp.max(jnp.maximum(near, far), axis=0, keepdims=True)
    count = jnp.int32(0)
    for place in range(LIST):
        used_ref[place] = 0
    for slot in range(SLOTS):
        used_ref[count] = slot
        count += (most[0, slot] > 0.0).astype(jnp.int32)
    used_ref[LIST] = count
    lane = iota((ROWS, 128), 1)
    turned = pltpu.roll(far, SAMPLES, 1)
    chosen = [
        jnp.where(lane == slot, near, jnp.where(lane == slot + SAMPLES, turned, 0.0))
        for slot in range(SLOTS)
    ]
    i, j, same = same_half()
    steps = add_lanes(jnp.concatenate(chosen, axis=0), same == (i % 2 == 0))
    step_ref[...] = steps.reshape(SLOTS, ROWS, 128)
    out_ref[...] = jnp.zeros((4, SLOTS, ROWS, 128), f32)

    def network(enc_ref, slot):
        first = w_ref[slot // CAP]
        head = head_ref[slot // CAP]
        for n in range(TILE // FORWARD_CHUNK):
            encoded = enc_ref[:, n * FORWARD_CHUNK : (n + 1) * FORWARD_CHUNK]
            half = jnp.dot(first, encoded, preferred_element_type=f32)
            hidden = (half + half * jnp.tanh(half)).astype(bf16)
            output = jnp.dot(head, hidden, preferred_element_type=f32)
            for r in range(FORWARD_CHUNK // 128):
                row = n * (FORWARD_CHUNK // 128) + r
                for v in range(4):
                    out_ref[v, slot, row : row + 1, :] = output[
                        12 + v : 13 + v, 128 * r : 128 * r + 128
                    ]

    wave_ref[...] = jnp.zeros(wave_ref.shape, f32)

    def prepare(ref, slot):
        encode_into(ref, kept_ref, wave_ref, recv_ref, slot)

    in_turns(used_ref, count, prepare, network, (enc_ref, next_ref))

    rows = SLOTS * ROWS
    outputs = [out_ref[v].reshape(rows, 128) for v in range(4)]
    raw = outputs[0]
    density = jnp.maximum(raw, 0.0) + jnp.log1p(jnp.exp(-jnp.abs(raw)))
    optical = density * steps
    inclusive = add_lanes(optical, same & (i <= j))
    leaving = jnp.exp(-inclusive)
    weight = jnp.exp(optical - inclusive) - leaving
    saved_ref[3] = jax.nn.sigmoid(raw).reshape(SLOTS, ROWS, 128)
    saved_ref[4] = weight.reshape(SLOTS, ROWS, 128)
    saved_ref[5] = leaving.reshape(SLOTS, ROWS, 128)
    i = iota((128, 256), 0)
    first_half = iota((128, 256), 1) < 128
    results = []
    for v in range(3):
        colour = jax.nn.sigmoid(outputs[1 + v])
        saved_ref[v] = colour.reshape(SLOTS, ROWS, 128)
        results.append(add_lanes(weight * colour, (i < SAMPLES) == first_half))
    results.append(add_lanes(leaving, i == jnp.where(first_half, SAMPLES - 1, 127)))
    for side in range(2):
        gathered = jnp.zeros((ROWS, 128), f32)
        for v in range(4):
            for slot in range(SLOTS):
                half = (side + slot) % 2
                block = results[v][slot * ROWS : (slot + 1) * ROWS, 128 * half : 128 * half + 128]
                gathered = jnp.where(lane == v * SLOTS + slot, block, gathered)
        small_ref[side * ROWS : (side + 1) * ROWS, :] = gathered


def forward(received, weights):
    vmem = pl.BlockSpec(memory_space=pltpu.VMEM)
    smem = pl.BlockSpec(memory_space=pltpu.SMEM)
    return pl.pallas_call(
        forward_kernel,
        out_shape=(
            jax.ShapeDtypeStruct((PEERS, 128), f32),
            jax.ShapeDtypeStruct((6, SLOTS, ROWS, 128), f32),
            jax.ShapeDtypeStruct((SLOTS, ROWS, 128), f32),
            jax.ShapeDtypeStruct((SLOTS, 64, TILE), bf16),
            jax.ShapeDtypeStruct((LIST + 1,), jnp.int32),
        ),
        in_specs=[vmem] * (1 + GROUP),
        out_specs=(vmem, vmem, vmem, vmem, smem),
        scratch_shapes=[
            pltpu.VMEM((GROUP, HIDDEN, 64), bf16),
            pltpu.VMEM((GROUP, 16, HIDDEN), bf16),
            pltpu.VMEM((64, TILE), bf16),
            pltpu.VMEM((64, TILE), bf16),
            pltpu.VMEM((64 * PITCH, 128), f32),
            pltpu.VMEM((4, SLOTS, ROWS, 128), f32),
        ],
        compiler_params=pltpu.CompilerParams(vmem_limit_bytes=SOME_VMEM),
        cost_estimate=matrix_cost(SLOTS * 2),
        name="forward",
    )(received, *weights)


def ray_kernel(small_ref, index_ref, dest_ref, target_ref, grads_ref, rendered_ref):
    lane = iota((ENTRIES, 128), 1)
    value = lane // SLOTS
    slot = (lane - value * SLOTS).astype(f32)
    dest_col = index_ref[:, 0:1]
    slot_col = index_ref[:, 64:65]
    to_entry = jnp.where(lane.astype(f32) == dest_col, 1.0, 0.0).astype(bf16)
    small = jnp.concatenate([small_ref[...], jnp.zeros((128 - PEERS, 128), f32)], axis=0)
    mine = (slot == slot_col) & (value < 4)
    found = jnp.where(mine, pick(to_entry, small), 0.0)
    i = iota((128, 128), 0)
    j = iota((128, 128), 1)
    segments = add_lanes(found, (i // SLOTS == j) & (j < 4))

    lane = iota((RAYS, 128), 1)
    parts = [segments[s * RAYS : (s + 1) * RAYS] for s in range(SEGS)]
    trans = [jnp.broadcast_to(part[:, 3:4], (RAYS, 128)) for part in parts]
    prefix = [jnp.ones((RAYS, 128), f32)]
    for s in range(SEGS - 1):
        prefix.append(prefix[s] * trans[s])
    rendered = prefix[0] * parts[0]
    for s in range(1, SEGS):
        rendered += prefix[s] * parts[s]
    target = jnp.concatenate([target_ref[...], jnp.zeros((3, 128 - RAYS), f32)], axis=1)
    target = jnp.concatenate([target, jnp.zeros((125, 128), f32)], axis=0).T[:RAYS]
    residual = jnp.where(lane < 3, rendered - target, 0.0)
    behind = jnp.zeros((RAYS, 128), f32)
    grads = [None] * SEGS
    for s in range(SEGS - 1, -1, -1):
        through = prefix[s] * jnp.sum(behind * residual, axis=1, keepdims=True)
        grads[s] = jnp.where(lane == 3, through, prefix[s] * residual)
        behind = parts[s] + trans[s] * behind
    spread_back = add_lanes(jnp.concatenate(grads, axis=0), (j // SLOTS == i) & (i < 4))
    to_dest = jnp.where(iota((PEERS, ENTRIES), 0).astype(f32) == dest_ref[0:1, :], 1.0, 0.0)
    grads_ref[...] = pick(to_dest.astype(bf16), jnp.where(mine, spread_back, 0.0))
    eye = as_matrix(iota((8, 128), 0) == iota((8, 128), 1))
    rendered_ref[...] = nt_dot(eye, rendered, lax.Precision.HIGHEST)[0:3]


def ray_level(small, index, dest, target):
    return pl.pallas_call(
        ray_kernel,
        out_shape=(
            jax.ShapeDtypeStruct((PEERS, 128), f32),
            jax.ShapeDtypeStruct((3, RAYS), f32),
        ),
        compiler_params=pltpu.CompilerParams(vmem_limit_bytes=SOME_VMEM),
        name="rays",
    )(small, index, dest, target)


def upstream_into(up_ref, grads_ref, saved_ref, step_ref):
    near = grads_ref[:ROWS]
    far = grads_ref[ROWS:]
    for v in range(4):
        for slot in range(SLOTS):
            up_ref[v, slot] = spread(near, far, slot, v * SLOTS + slot)

    rows = SLOTS * ROWS

    def flat(x):
        return x.reshape(rows, 128)

    i, j, same = same_half()
    weight = flat(saved_ref[4])
    leaving = flat(saved_ref[5])
    shading = flat(saved_ref[0]) * flat(up_ref[0])
    shading += flat(saved_ref[1]) * flat(up_ref[1])
    shading += flat(saved_ref[2]) * flat(up_ref[2])
    after = add_lanes(weight * shading, same & (i > j))
    last = add_lanes(leaving, same & ((i == SAMPLES - 1) | (i == 127)))
    grad_depth = shading * leaving - after - flat(up_ref[3]) * last
    upstream = [grad_depth * flat(step_ref[...]) * flat(saved_ref[3])]
    for v in range(3):
        colour = flat(saved_ref[v])
        upstream.append(weight * flat(up_ref[v]) * colour * (1.0 - colour))
    for v in range(4):
        up_ref[v] = upstream[v].reshape(SLOTS, ROWS, 128)


def backward_kernel(*refs):
    member_ref, grads_ref, saved_ref, step_ref, kept_ref, used_ref = refs[:6]
    weight_refs = refs[6 : 6 + GROUP]
    total_ref, up_ref, both_ref, first_ref, head_ref, *buffers = refs[6 + GROUP :]
    input_ref, next_ref, wave_ref, before_ref, hidden_ref = buffers
    both_ref[...] = jnp.zeros(both_ref.shape, bf16)
    for i in range(GROUP):
        packed = (0.5 * weight_refs[i][...]).astype(bf16)
        both_ref[i, :64, :HIDDEN] = packed
        both_ref[i, 64:, HIDDEN:] = packed[48:]
    first_ref[...] = jnp.zeros(first_ref.shape, f32)
    head_ref[...] = jnp.zeros(head_ref.shape, f32)
    upstream_into(up_ref, grads_ref, saved_ref, step_ref)
    wave_ref[...] = jnp.zeros(wave_ref.shape, f32)

    def prepare(ref, slot):
        for v in range(4):
            put_row(wave_ref, 12 + v, up_ref[v, slot])
        for r in range(ROWS):
            ref[:, 128 * r : 128 * r + 128] = wave_ref[pl.ds(r, 16, stride=PITCH), :].astype(bf16)

    def work(ref, slot):
        brick = slot // CAP
        both = both_ref[brick]
        for n in range(TILE // BACKWARD_CHUNK):
            chunk = slice(n * BACKWARD_CHUNK, (n + 1) * BACKWARD_CHUNK)
            given = jnp.concatenate([kept_ref[slot, :, chunk], ref[:, chunk]], axis=0)
            product = tn_dot(given, both)
            half = product[:, :HIDDEN]
            bend = jnp.tanh(half)
            bent = half * bend
            slope = (1.0 + bend) * ((1.0 + half) - bent)
            hidden_ref[chunk] = (half + bent).astype(bf16)
            before_ref[chunk] = (product[:, HIDDEN:] * slope).astype(bf16)
        first_ref[brick] += jnp.dot(kept_ref[slot], before_ref[...], preferred_element_type=f32)
        head_ref[brick] += jnp.dot(ref[...], hidden_ref[...], preferred_element_type=f32)

    in_turns(used_ref, used_ref[LIST], prepare, work, (input_ref, next_ref))
    for i in range(GROUP):
        member = lax.rem(member_ref[0] + i, GROUP)
        total_ref[member, :48] = first_ref[i, :48]
        total_ref[member, 48:] = first_ref[i, 48:] + head_ref[i]


def backward(member, grads, saved, steps, kept, used, weights):
    vmem = pl.BlockSpec(memory_space=pltpu.VMEM)
    smem = pl.BlockSpec(memory_space=pltpu.SMEM)
    return pl.pallas_call(
        backward_kernel,
        out_shape=jax.ShapeDtypeStruct((GROUP, 64, HIDDEN), f32),
        in_specs=[smem, vmem, vmem, vmem, vmem, smem] + [vmem] * GROUP,
        out_specs=vmem,
        scratch_shapes=[
            pltpu.VMEM((4, SLOTS, ROWS, 128), f32),
            pltpu.VMEM((GROUP, 80, 2 * HIDDEN), bf16),
            pltpu.VMEM((GROUP, 64, HIDDEN), f32),
            pltpu.VMEM((GROUP, 16, HIDDEN), f32),
            pltpu.VMEM((16, TILE), bf16),
            pltpu.VMEM((16, TILE), bf16),
            pltpu.VMEM((16 * PITCH, 128), f32),
            pltpu.VMEM((TILE, HIDDEN), bf16),
            pltpu.VMEM((TILE, HIDDEN), bf16),
        ],
        compiler_params=pltpu.CompilerParams(vmem_limit_bytes=SOME_VMEM),
        cost_estimate=matrix_cost(SLOTS * 4),
        name="backward",
    )(member, grads, saved, steps, kept, used, *weights)


def sum_kernel(*refs):
    parts_ref, total_ref, square_ref = refs
    total = parts_ref[0]
    for i in range(1, GROUP):
        total += parts_ref[i]
    total_ref[...] = total
    square = jnp.sum(jnp.sum(total * total, axis=1, keepdims=True), axis=0, keepdims=True)
    square_ref[...] = jnp.broadcast_to(square, square_ref.shape)


def add_up(partials, bricks):
    return pl.pallas_call(
        sum_kernel,
        out_shape=(
            jax.ShapeDtypeStruct((64, HIDDEN), f32),
            jax.ShapeDtypeStruct((bricks, 128), f32),
        ),
        compiler_params=pltpu.CompilerParams(vmem_limit_bytes=SOME_VMEM),
        name="add_up",
    )(partials)


def normalize(total, squares, count):
    def body(total_ref, squares_ref, first_ref, head_ref):
        overall = jnp.sum(squares_ref[:, 0:1], axis=0, keepdims=True)
        scaled = total_ref[...] * lax.rsqrt(overall / count + NORM_EPS)
        first_ref[:, 0, :] = scaled[: 6 * FREQS]
        head_ref[0] = scaled[6 * FREQS :]

    first, head = pl.pallas_call(
        body,
        out_shape=(
            jax.ShapeDtypeStruct((6 * FREQS, 1, HIDDEN), f32),
            jax.ShapeDtypeStruct((1, 4, HIDDEN), f32),
        ),
        compiler_params=pltpu.CompilerParams(vmem_limit_bytes=SOME_VMEM),
        name="normalize",
    )(total, squares)
    return first.transpose(1, 2, 0), head


def from_ahead(x, distance):
    return lax.ppermute(x, GROUP_AXIS, [(i, (i - distance) % GROUP) for i in range(GROUP)])


def exchange(x, axes):
    return lax.all_to_all(x, axes, split_axis=0, concat_axis=0, tiled=True)


def on_device(positions, spacing, crossings, target, first_weight, head_weight):
    own = jnp.concatenate(
        [first_weight[0].astype(f32).T, head_weight[0].astype(f32)], axis=0
    )
    weights = [own] + [from_ahead(own, distance) for distance in range(1, GROUP)]
    bricks = GROUP * PEERS
    member = lax.axis_index(GROUP_AXIS).astype(jnp.int32).reshape(1)
    peer = lax.axis_index(PEER_AXES).astype(jnp.int32).reshape(1)
    send, index, dest = pack(member, peer, positions, spacing.T, crossings.T)
    received = exchange(send, PEER_AXES)
    small, saved, steps, kept, used = forward(received, weights)
    grads, rendered = ray_level(exchange(small, PEER_AXES), index, dest, target)
    grads = exchange(grads, PEER_AXES)
    partials = backward(member, grads, saved, steps, kept, used, weights)
    total, square = add_up(exchange(partials, GROUP_AXIS), bricks)
    squares = exchange(square, ALL)
    first_update, head_update = normalize(total, squares, bricks * (64 * HIDDEN))
    return (rendered, first_update, head_update)


def solution(mesh):
    in_specs = (
        P(None, ALL, None),
        P(ALL, None),
        P(ALL, None),
        P(None, ALL),
        P(ALL, None, None),
        P(ALL, None, None),
    )
    out_specs = (P(None, ALL), P(ALL, None, None), P(ALL, None, None))
    return jax.shard_map(
        on_device, mesh=mesh, in_specs=in_specs, out_specs=out_specs, check_vma=False
    )
```

```python
import jax
import jax.numpy as jnp
from jax import lax
from jax.experimental import pallas as pl
from jax.experimental.pallas import tpu as pltpu
from jax.sharding import PartitionSpec as P

FREQS = 10
SAMPLES = 64
SEGS = 8
CAP = 3
ANCHOR = 5
NORM_EPS = 1e-06

RAYS = 48
GROUP = 8
PEERS = 32
SLOTS = GROUP * CAP
PAIRS = SLOTS // 2
ROWS = PEERS // 2
PITCH = ROWS + 1
TILE = PEERS * SAMPLES
ENTRIES = RAYS * SEGS
LIST = SLOTS + 2
STEP_ROW = 3 * PAIRS
WIRE = STEP_ROW + 1
HIDDEN = 256
FORWARD_CHUNK = 2048
BACKWARD_CHUNK = 512
VMEM = 56 * 1024 * 1024
SOME_VMEM = 24 * 1024 * 1024
ALL = ("gx", "gy", "gz")
PEER_AXES = ("gx", "gy")
GROUP_AXIS = "gz"

SIN_TERMS = (
    6.283185160116253,
    -41.34165503574907,
    81.60100428250003,
    -76.54978619700827,
    39.536730859838705,
)

f32 = jnp.float32
bf16 = jnp.bfloat16


def iota(shape, dim):
    return lax.broadcasted_iota(jnp.int32, shape, dim)


def nt_dot(a, b, precision=None):
    return lax.dot_general(
        a, b, (((1,), (1,)), ((), ())), preferred_element_type=f32, precision=precision
    )


def tn_dot(a, b):
    return lax.dot_general(a, b, (((0,), (0,)), ((), ())), preferred_element_type=f32)


def matrix_cost(tile_passes):
    return pl.CostEstimate(
        flops=tile_passes * 2 * HIDDEN * HIDDEN * TILE, bytes_accessed=4 << 20, transcendentals=0
    )


def wire_row(row):
    return pl.ds(128 * row if isinstance(row, int) else pl.multiple_of(128 * row, 128), 128)


def split3(x):
    high = x.astype(bf16)
    rest = x - high.astype(f32)
    mid = rest.astype(bf16)
    return high, mid, (rest - mid.astype(f32)).astype(bf16)


def pick(one_hot, x):
    high, mid, low = split3(x)
    total = jnp.dot(one_hot, low, preferred_element_type=f32)
    total += jnp.dot(one_hot, mid, preferred_element_type=f32)
    return total + jnp.dot(one_hot, high, preferred_element_type=f32)


def add_lanes(x, mask):
    ones = as_matrix(mask).astype(bf16)
    high, mid, low = split3(x)
    total = jnp.dot(low, ones, preferred_element_type=f32)
    total += jnp.dot(mid, ones, preferred_element_type=f32)
    return total + jnp.dot(high, ones, preferred_element_type=f32)


def column_of(rows_ref):
    rows = rows_ref[...].astype(f32)
    padded = jnp.concatenate([rows, jnp.zeros((SEGS, 128 - RAYS), f32)], axis=1).T
    return jnp.concatenate([padded[:RAYS, s : s + 1] for s in range(SEGS)], axis=0)


def pack_kernel(
    member_ref, peer_ref, pos_ref, step_ref, cross_ref, send_ref, index_ref, dest_ref, data_ref
):
    brick_col = column_of(cross_ref)
    step_col = column_of(step_ref)
    sub = iota((ENTRIES, ENTRIES), 0)
    lane = iota((ENTRIES, ENTRIES), 1)
    brick_row = jnp.sum(jnp.where(sub == lane, brick_col, 0.0), axis=0, keepdims=True)
    same = brick_col == brick_row
    rank_col = jnp.sum(jnp.where(same & (lane < sub), 1.0, 0.0), axis=1, keepdims=True)
    rank_row = jnp.sum(jnp.where(same & (sub < lane), 1.0, 0.0), axis=0, keepdims=True)
    own = member_ref[0].astype(f32)

    def place(number, rank):
        dest = jnp.floor(number * (1.0 / GROUP))
        ahead = number - GROUP * dest - own
        ahead = jnp.where(ahead < 0.0, ahead + GROUP, ahead)
        return dest, ahead * CAP + rank

    dest_col, slot_col = place(brick_col, rank_col)
    dest_row, slot_row = place(brick_row, rank_row)
    pair_row = jnp.floor(slot_row * 0.5)
    half_row = slot_row - 2.0 * pair_row
    half_row = jnp.where(peer_ref[0] < ROWS, half_row, 1.0 - half_row)
    target_row = pair_row * PEERS + dest_row
    here = sub.astype(f32) == target_row
    one_hot = jnp.concatenate(
        [jnp.where(here & (half_row == half), 1.0, 0.0).astype(bf16) for half in (0.0, 1.0)], axis=1
    )
    left = iota((RAYS, 128), 1) < SAMPLES
    for c in range(3):
        for q in range(SEGS // 2):
            x = pos_ref[c, :, 128 * q : 128 * q + 128]
            y = pltpu.roll(x, SAMPLES, 1)
            blocks = (
                (0, 2 * q, jnp.where(left, x, 0.0)),
                (0, 2 * q + 1, jnp.where(left, y, 0.0)),
                (1, 2 * q, jnp.where(left, 0.0, y)),
                (1, 2 * q + 1, jnp.where(left, 0.0, x)),
            )
            for half, s, block in blocks:
                row = half * ENTRIES + s * RAYS
                for part, value in enumerate(split3(block)):
                    data_ref[part, row : row + RAYS, 128 * c : 128 * c + 128] = value
    total = jnp.dot(one_hot, data_ref[2], preferred_element_type=f32)
    total += jnp.dot(one_hot, data_ref[1], preferred_element_type=f32)
    total += jnp.dot(one_hot, data_ref[0], preferred_element_type=f32)
    for pair in range(PAIRS):
        for c in range(3):
            send_ref[:, 0, wire_row(3 * pair + c)] = total[
                pair * PEERS : (pair + 1) * PEERS, 128 * c : 128 * c + 128
            ]
    to_dest = jnp.where(iota((PEERS, ENTRIES), 0).astype(f32) == dest_row, 1.0, 0.0)
    lane_128 = iota((ENTRIES, 128), 1)
    by_slot = jnp.where(lane_128.astype(f32) == slot_col, step_col, 0.0)
    send_ref[:, 0, wire_row(STEP_ROW)] = pick(to_dest.astype(bf16), by_slot)
    index_ref[...] = jnp.where(lane_128 < 64, dest_col, slot_col)
    dest_ref[...] = jnp.broadcast_to(dest_row, (8, ENTRIES))


def pack(member, peer, positions, spacing, crossings):
    vmem = pl.BlockSpec(memory_space=pltpu.VMEM)
    smem = pl.BlockSpec(memory_space=pltpu.SMEM)
    return pl.pallas_call(
        pack_kernel,
        out_shape=(
            jax.ShapeDtypeStruct((PEERS, 1, 128 * WIRE), f32),
            jax.ShapeDtypeStruct((ENTRIES, 128), f32),
            jax.ShapeDtypeStruct((8, ENTRIES), f32),
        ),
        in_specs=[smem, smem, vmem, vmem, vmem],
        out_specs=(vmem, vmem, vmem),
        scratch_shapes=[pltpu.VMEM((3, 2 * ENTRIES, 384), bf16)],
        compiler_params=pltpu.CompilerParams(vmem_limit_bytes=VMEM),
        name="pack",
    )(member, peer, positions, spacing, crossings)


def sine_of_turns(y):
    z = y * y
    value = SIN_TERMS[-1]
    for term in SIN_TERMS[-2::-1]:
        value = value * z + term
    return value * y


def put_row(wave_ref, row, values):
    wave_ref[row * PITCH : row * PITCH + ROWS, :] = values


def encode_into(enc_ref, kept_ref, wave_ref, recv_ref, slot):
    pair = slot // 2
    near_side = (iota((ROWS, 128), 1) < SAMPLES) == (slot == 2 * pair)
    points = jnp.concatenate(
        [
            jnp.where(
                near_side,
                recv_ref[:ROWS, 0, wire_row(3 * pair + c)],
                recv_ref[ROWS:, 0, wire_row(3 * pair + c)],
            )
            for c in range(3)
        ],
        axis=0,
    )
    for k in range(FREQS):
        if k % ANCHOR == 0:
            turns = points * (0.5 * 2.0**k)
            turns = turns - jnp.round(turns)
            size = jnp.abs(turns)
            cosine = sine_of_turns(0.25 - size)
            sine = sine_of_turns(jnp.minimum(size, 0.5 - size))
            sine = jnp.where(turns < 0.0, -sine, sine)
        else:
            square = sine * sine
            sine = sine * cosine
            sine = sine + sine
            cosine = 1.0 - (square + square)
        for c in range(3):
            put_row(wave_ref, 6 * k + c, sine[c * ROWS : (c + 1) * ROWS])
            put_row(wave_ref, 6 * k + 3 + c, cosine[c * ROWS : (c + 1) * ROWS])
    for r in range(ROWS):
        lanes = slice(128 * r, 128 * r + 128)
        waves = wave_ref[pl.ds(r, 64, stride=PITCH), :].astype(bf16)
        enc_ref[:, lanes] = waves
        kept_ref[slot, :, lanes] = waves


def in_turns(used_ref, count, prepare, work, buffers, work_first=False):
    here, other = buffers
    prepare(here, used_ref[0])

    def both(empty, later, full, now):
        if work_first:
            work(full, now)
        prepare(empty, later)
        if not work_first:
            work(full, now)

    def turn(number, carry):
        place = 2 * number
        both(other, used_ref[place + 1], here, used_ref[place])

        @pl.when(place + 1 < count)
        def _():
            both(here, used_ref[place + 2], other, used_ref[place + 1])

        return carry

    lax.fori_loop(0, (count + 1) // 2, turn, 0)


def spread(near, far, slot, lane_index):
    near_side = (iota((ROWS, 128), 1) < SAMPLES) == (slot % 2 == 0)
    return jnp.where(
        near_side, near[:, lane_index : lane_index + 1], far[:, lane_index : lane_index + 1]
    )


def same_half():
    i = iota((128, 128), 0)
    j = iota((128, 128), 1)
    return i, j, (i < SAMPLES) == (j < SAMPLES)


def as_matrix(mask):
    return jnp.where(mask, 1.0, 0.0)


def forward_kernel(*refs):
    recv_ref = refs[0]
    weight_refs = refs[1 : 1 + GROUP]
    small_ref, saved_ref, step_ref, kept_ref, used_ref = refs[1 + GROUP : 6 + GROUP]
    w_ref, head_ref, enc_ref, next_ref, wave_ref, out_ref = refs[6 + GROUP :]

    for i in range(GROUP):
        packed = weight_refs[i][...]
        w_ref[i] = (0.5 * packed).T.astype(bf16)
        head_ref[i] = packed[48:64].astype(bf16)

    near = recv_ref[:ROWS, 0, wire_row(STEP_ROW)]
    far = recv_ref[ROWS:, 0, wire_row(STEP_ROW)]
    most = jnp.max(jnp.maximum(near, far), axis=0, keepdims=True)
    count = jnp.int32(0)
    for place in range(LIST):
        used_ref[place] = 0
    for slot in range(SLOTS):
        used_ref[count] = slot
        count += (most[0, slot] > 0.0).astype(jnp.int32)
    used_ref[LIST] = count
    lane = iota((ROWS, 128), 1)
    turned = pltpu.roll(far, SAMPLES, 1)
    chosen = [
        jnp.where(lane == slot, near, jnp.where(lane == slot + SAMPLES, turned, 0.0))
        for slot in range(SLOTS)
    ]
    i, j, same = same_half()
    steps = add_lanes(jnp.concatenate(chosen, axis=0), same == (i % 2 == 0))
    step_ref[...] = steps.reshape(SLOTS, ROWS, 128)
    out_ref[...] = jnp.zeros((4, SLOTS, ROWS, 128), f32)

    def network(enc_ref, slot):
        first = w_ref[slot // CAP]
        head = head_ref[slot // CAP]
        for n in range(TILE // FORWARD_CHUNK):
            encoded = enc_ref[:, n * FORWARD_CHUNK : (n + 1) * FORWARD_CHUNK]
            half = jnp.dot(first, encoded, preferred_element_type=f32)
            hidden = (half + half * jnp.tanh(half)).astype(bf16)
            output = jnp.dot(head, hidden, preferred_element_type=f32)
            for r in range(FORWARD_CHUNK // 128):
                row = n * (FORWARD_CHUNK // 128) + r
                for v in range(4):
                    out_ref[v, slot, row : row + 1, :] = output[
                        12 + v : 13 + v, 128 * r : 128 * r + 128
                    ]

    wave_ref[...] = jnp.zeros(wave_ref.shape, f32)

    def prepare(ref, slot):
        encode_into(ref, kept_ref, wave_ref, recv_ref, slot)

    in_turns(used_ref, count, prepare, network, (enc_ref, next_ref), work_first=True)

    rows = SLOTS * ROWS
    outputs = [out_ref[v].reshape(rows, 128) for v in range(4)]
    raw = outputs[0]
    density = jnp.maximum(raw, 0.0) + jnp.log1p(jnp.exp(-jnp.abs(raw)))
    optical = density * steps
    inclusive = add_lanes(optical, same & (i <= j))
    leaving = jnp.exp(-inclusive)
    weight = jnp.exp(optical - inclusive) - leaving
    saved_ref[3] = jax.nn.sigmoid(raw).reshape(SLOTS, ROWS, 128)
    saved_ref[4] = weight.reshape(SLOTS, ROWS, 128)
    saved_ref[5] = leaving.reshape(SLOTS, ROWS, 128)
    i = iota((128, 256), 0)
    first_half = iota((128, 256), 1) < 128
    results = []
    for v in range(3):
        colour = jax.nn.sigmoid(outputs[1 + v])
        saved_ref[v] = colour.reshape(SLOTS, ROWS, 128)
        results.append(add_lanes(weight * colour, (i < SAMPLES) == first_half))
    results.append(add_lanes(leaving, i == jnp.where(first_half, SAMPLES - 1, 127)))
    for side in range(2):
        gathered = jnp.zeros((ROWS, 128), f32)
        for v in range(4):
            for slot in range(SLOTS):
                half = (side + slot) % 2
                block = results[v][slot * ROWS : (slot + 1) * ROWS, 128 * half : 128 * half + 128]
                gathered = jnp.where(lane == v * SLOTS + slot, block, gathered)
        small_ref[side * ROWS : (side + 1) * ROWS, :] = gathered


def forward(received, weights):
    vmem = pl.BlockSpec(memory_space=pltpu.VMEM)
    smem = pl.BlockSpec(memory_space=pltpu.SMEM)
    return pl.pallas_call(
        forward_kernel,
        out_shape=(
            jax.ShapeDtypeStruct((PEERS, 128), f32),
            jax.ShapeDtypeStruct((6, SLOTS, ROWS, 128), f32),
            jax.ShapeDtypeStruct((SLOTS, ROWS, 128), f32),
            jax.ShapeDtypeStruct((SLOTS, 64, TILE), bf16),
            jax.ShapeDtypeStruct((LIST + 1,), jnp.int32),
        ),
        in_specs=[vmem] * (1 + GROUP),
        out_specs=(vmem, vmem, vmem, vmem, smem),
        scratch_shapes=[
            pltpu.VMEM((GROUP, HIDDEN, 64), bf16),
            pltpu.VMEM((GROUP, 16, HIDDEN), bf16),
            pltpu.VMEM((64, TILE), bf16),
            pltpu.VMEM((64, TILE), bf16),
            pltpu.VMEM((64 * PITCH, 128), f32),
            pltpu.VMEM((4, SLOTS, ROWS, 128), f32),
        ],
        compiler_params=pltpu.CompilerParams(vmem_limit_bytes=SOME_VMEM),
        cost_estimate=matrix_cost(SLOTS * 2),
        name="forward",
    )(received, *weights)


def ray_kernel(small_ref, index_ref, dest_ref, target_ref, grads_ref, rendered_ref):
    lane = iota((ENTRIES, 128), 1)
    value = lane // SLOTS
    slot = (lane - value * SLOTS).astype(f32)
    dest_col = index_ref[:, 0:1]
    slot_col = index_ref[:, 64:65]
    to_entry = jnp.where(lane.astype(f32) == dest_col, 1.0, 0.0).astype(bf16)
    small = jnp.concatenate([small_ref[...], jnp.zeros((128 - PEERS, 128), f32)], axis=0)
    mine = (slot == slot_col) & (value < 4)
    found = jnp.where(mine, pick(to_entry, small), 0.0)
    i = iota((128, 128), 0)
    j = iota((128, 128), 1)
    segments = add_lanes(found, (i // SLOTS == j) & (j < 4))

    lane = iota((RAYS, 128), 1)
    parts = [segments[s * RAYS : (s + 1) * RAYS] for s in range(SEGS)]
    trans = [jnp.broadcast_to(part[:, 3:4], (RAYS, 128)) for part in parts]
    prefix = [jnp.ones((RAYS, 128), f32)]
    for s in range(SEGS - 1):
        prefix.append(prefix[s] * trans[s])
    rendered = prefix[0] * parts[0]
    for s in range(1, SEGS):
        rendered += prefix[s] * parts[s]
    target = jnp.concatenate([target_ref[...], jnp.zeros((3, 128 - RAYS), f32)], axis=1)
    target = jnp.concatenate([target, jnp.zeros((125, 128), f32)], axis=0).T[:RAYS]
    residual = jnp.where(lane < 3, rendered - target, 0.0)
    behind = jnp.zeros((RAYS, 128), f32)
    grads = [None] * SEGS
    for s in range(SEGS - 1, -1, -1):
        through = prefix[s] * jnp.sum(behind * residual, axis=1, keepdims=True)
        grads[s] = jnp.where(lane == 3, through, prefix[s] * residual)
        behind = parts[s] + trans[s] * behind
    spread_back = add_lanes(jnp.concatenate(grads, axis=0), (j // SLOTS == i) & (i < 4))
    to_dest = jnp.where(iota((PEERS, ENTRIES), 0).astype(f32) == dest_ref[0:1, :], 1.0, 0.0)
    grads_ref[...] = pick(to_dest.astype(bf16), jnp.where(mine, spread_back, 0.0))
    eye = as_matrix(iota((8, 128), 0) == iota((8, 128), 1))
    rendered_ref[...] = nt_dot(eye, rendered, lax.Precision.HIGHEST)[0:3]


def ray_level(small, index, dest, target):
    return pl.pallas_call(
        ray_kernel,
        out_shape=(
            jax.ShapeDtypeStruct((PEERS, 128), f32),
            jax.ShapeDtypeStruct((3, RAYS), f32),
        ),
        compiler_params=pltpu.CompilerParams(vmem_limit_bytes=SOME_VMEM),
        name="rays",
    )(small, index, dest, target)


def upstream_into(up_ref, grads_ref, saved_ref, step_ref):
    near = grads_ref[:ROWS]
    far = grads_ref[ROWS:]
    for v in range(4):
        for slot in range(SLOTS):
            up_ref[v, slot] = spread(near, far, slot, v * SLOTS + slot)

    rows = SLOTS * ROWS

    def flat(x):
        return x.reshape(rows, 128)

    i, j, same = same_half()
    weight = flat(saved_ref[4])
    leaving = flat(saved_ref[5])
    shading = flat(saved_ref[0]) * flat(up_ref[0])
    shading += flat(saved_ref[1]) * flat(up_ref[1])
    shading += flat(saved_ref[2]) * flat(up_ref[2])
    after = add_lanes(weight * shading, same & (i > j))
    last = add_lanes(leaving, same & ((i == SAMPLES - 1) | (i == 127)))
    grad_depth = shading * leaving - after - flat(up_ref[3]) * last
    upstream = [grad_depth * flat(step_ref[...]) * flat(saved_ref[3])]
    for v in range(3):
        colour = flat(saved_ref[v])
        upstream.append(weight * flat(up_ref[v]) * colour * (1.0 - colour))
    for v in range(4):
        up_ref[v] = upstream[v].reshape(SLOTS, ROWS, 128)


def backward_kernel(*refs):
    member_ref, grads_ref, saved_ref, step_ref, kept_ref, used_ref = refs[:6]
    weight_refs = refs[6 : 6 + GROUP]
    total_ref, up_ref, both_ref, first_ref, head_ref, *buffers = refs[6 + GROUP :]
    input_ref, next_ref, wave_ref, before_ref, hidden_ref = buffers
    both_ref[...] = jnp.zeros(both_ref.shape, bf16)
    for i in range(GROUP):
        packed = (0.5 * weight_refs[i][...]).astype(bf16)
        both_ref[i, :64, :HIDDEN] = packed
        both_ref[i, 64:, HIDDEN:] = packed[48:]
    first_ref[...] = jnp.zeros(first_ref.shape, f32)
    head_ref[...] = jnp.zeros(head_ref.shape, f32)
    upstream_into(up_ref, grads_ref, saved_ref, step_ref)
    wave_ref[...] = jnp.zeros(wave_ref.shape, f32)

    def prepare(ref, slot):
        for v in range(4):
            put_row(wave_ref, 12 + v, up_ref[v, slot])
        for r in range(ROWS):
            ref[:, 128 * r : 128 * r + 128] = wave_ref[pl.ds(r, 16, stride=PITCH), :].astype(bf16)

    def work(ref, slot):
        brick = slot // CAP
        both = both_ref[brick]
        for n in range(TILE // BACKWARD_CHUNK):
            chunk = slice(n * BACKWARD_CHUNK, (n + 1) * BACKWARD_CHUNK)
            given = jnp.concatenate([kept_ref[slot, :, chunk], ref[:, chunk]], axis=0)
            product = tn_dot(given, both)
            half = product[:, :HIDDEN]
            bend = jnp.tanh(half)
            bent = half * bend
            slope = (1.0 + bend) * ((1.0 + half) - bent)
            hidden_ref[chunk] = (half + bent).astype(bf16)
            before_ref[chunk] = (product[:, HIDDEN:] * slope).astype(bf16)
        first_ref[brick] += jnp.dot(kept_ref[slot], before_ref[...], preferred_element_type=f32)
        head_ref[brick] += jnp.dot(ref[...], hidden_ref[...], preferred_element_type=f32)

    in_turns(used_ref, used_ref[LIST], prepare, work, (input_ref, next_ref))
    for i in range(GROUP):
        member = lax.rem(member_ref[0] + i, GROUP)
        total_ref[member, :48] = first_ref[i, :48]
        total_ref[member, 48:] = first_ref[i, 48:] + head_ref[i]


def backward(member, grads, saved, steps, kept, used, weights):
    vmem = pl.BlockSpec(memory_space=pltpu.VMEM)
    smem = pl.BlockSpec(memory_space=pltpu.SMEM)
    return pl.pallas_call(
        backward_kernel,
        out_shape=jax.ShapeDtypeStruct((GROUP, 64, HIDDEN), f32),
        in_specs=[smem, vmem, vmem, vmem, vmem, smem] + [vmem] * GROUP,
        out_specs=vmem,
        scratch_shapes=[
            pltpu.VMEM((4, SLOTS, ROWS, 128), f32),
            pltpu.VMEM((GROUP, 80, 2 * HIDDEN), bf16),
            pltpu.VMEM((GROUP, 64, HIDDEN), f32),
            pltpu.VMEM((GROUP, 16, HIDDEN), f32),
            pltpu.VMEM((16, TILE), bf16),
            pltpu.VMEM((16, TILE), bf16),
            pltpu.VMEM((16 * PITCH, 128), f32),
            pltpu.VMEM((TILE, HIDDEN), bf16),
            pltpu.VMEM((TILE, HIDDEN), bf16),
        ],
        compiler_params=pltpu.CompilerParams(vmem_limit_bytes=SOME_VMEM),
        cost_estimate=matrix_cost(SLOTS * 4),
        name="backward",
    )(member, grads, saved, steps, kept, used, *weights)


def sum_kernel(*refs):
    parts_ref, total_ref, square_ref = refs
    total = parts_ref[0]
    for i in range(1, GROUP):
        total += parts_ref[i]
    total_ref[...] = total
    square = jnp.sum(jnp.sum(total * total, axis=1, keepdims=True), axis=0, keepdims=True)
    square_ref[...] = jnp.broadcast_to(square, square_ref.shape)


def add_up(partials, bricks):
    return pl.pallas_call(
        sum_kernel,
        out_shape=(
            jax.ShapeDtypeStruct((64, HIDDEN), f32),
            jax.ShapeDtypeStruct((bricks, 128), f32),
        ),
        compiler_params=pltpu.CompilerParams(vmem_limit_bytes=SOME_VMEM),
        name="add_up",
    )(partials)


def normalize(total, squares, count):
    def body(total_ref, squares_ref, first_ref, head_ref):
        overall = jnp.sum(squares_ref[:, 0:1], axis=0, keepdims=True)
        scaled = total_ref[...] * lax.rsqrt(overall / count + NORM_EPS)
        first_ref[:, 0, :] = scaled[: 6 * FREQS]
        head_ref[0] = scaled[6 * FREQS :]

    first, head = pl.pallas_call(
        body,
        out_shape=(
            jax.ShapeDtypeStruct((6 * FREQS, 1, HIDDEN), f32),
            jax.ShapeDtypeStruct((1, 4, HIDDEN), f32),
        ),
        compiler_params=pltpu.CompilerParams(vmem_limit_bytes=SOME_VMEM),
        name="normalize",
    )(total, squares)
    return first.transpose(1, 2, 0), head


def from_ahead(x, distance):
    return lax.ppermute(x, GROUP_AXIS, [(i, (i - distance) % GROUP) for i in range(GROUP)])


def exchange(x, axes):
    return lax.all_to_all(x, axes, split_axis=0, concat_axis=0, tiled=True)


def on_device(positions, spacing, crossings, target, first_weight, head_weight):
    own = jnp.concatenate(
        [first_weight[0].astype(f32).T, head_weight[0].astype(f32)], axis=0
    )
    weights = [own] + [from_ahead(own, distance) for distance in range(1, GROUP)]
    bricks = GROUP * PEERS
    member = lax.axis_index(GROUP_AXIS).astype(jnp.int32).reshape(1)
    peer = lax.axis_index(PEER_AXES).astype(jnp.int32).reshape(1)
    send, index, dest = pack(member, peer, positions, spacing.T, crossings.T)
    received = exchange(send, PEER_AXES)
    small, saved, steps, kept, used = forward(received, weights)
    grads, rendered = ray_level(exchange(small, PEER_AXES), index, dest, target)
    grads = exchange(grads, PEER_AXES)
    partials = backward(member, grads, saved, steps, kept, used, weights)
    total, square = add_up(exchange(partials, GROUP_AXIS), bricks)
    squares = exchange(square, ALL)
    first_update, head_update = normalize(total, squares, bricks * (64 * HIDDEN))
    return (rendered, first_update, head_update)


def solution(mesh):
    in_specs = (
        P(None, ALL, None),
        P(ALL, None),
        P(ALL, None),
        P(None, ALL),
        P(ALL, None, None),
        P(ALL, None, None),
    )
    out_specs = (P(None, ALL), P(ALL, None, None), P(ALL, None, None))
    return jax.shard_map(
        on_device, mesh=mesh, in_specs=in_specs, out_specs=out_specs, check_vma=False
    )
```
